128 devices in a mesh: enc: 4 (over y), fsdp: 32 (over z, x, core).
Axes of the slice: x: 4, y: 4, z: 4, core: 2. Of those that a mesh axis runs over, the one named last changes fastest.
Arguments:
- hidden: bfloat16 [24576, 4096], P(('enc', 'fsdp')), may hold values from -60 to 60
- query_weight: bfloat16 [4096, 2048], P('fsdp'), may hold values from -0.09375 to 0.09375
- neighbour_keys: bfloat16 [768, 128, 2048], P(('enc', 'fsdp')), may hold values from -50 to 50
- neighbour_values: bfloat16 [768, 128, 2048], P(('enc', 'fsdp')), may hold values from -6 to 6
- neighbour_owner: int32 [384, 2], P(('enc', 'fsdp')), may hold values from 0 to 3, all different within a row; in each aligned block of 3 rows (0 to 2, 3 to 5, ...) at most 2 rows name the same one
- neighbour_row: int32 [384, 2], P(('enc', 'fsdp')), may hold values from 0 to 5
- output_cotangent: bfloat16 [24576, 2048], P(('enc', 'fsdp')), may hold values from -6 to 6
Outputs:
- attended: bfloat16 [24576, 2048], P(('enc', 'fsdp'))
- grad_hidden: bfloat16 [24576, 4096], P(('enc', 'fsdp'))
- grad_keys: bfloat16 [768, 128, 2048], P(('enc', 'fsdp'))
- grad_values: bfloat16 [768, 128, 2048], P(('enc', 'fsdp'))
The draws below stay inside these ranges and needn't reach their ends.
Inputs may be any that keep to these rules, and one draw needn't show every extreme that they name: `neighbour_owner`: the two owners of a group differ. Among the 3 groups of one device (aligned blocks of rows), no owner is named more than 2 times.
All inputs are finite; a program needn't handle non-finite values.
Results may differ from the reference program's by a relative error of at most 0.012.
The reference program's roundings to bfloat16 on the way count: a program that leaves them out, or rounds other values in their place, can miss the bound.
Values may be sent and summed in bfloat16 or wider, within the bound.
No kernel may reach another device: no remote copies, remote signals or barrier semaphores. Data moves between devices by JAX's collectives and lax.ppermute only.
A program may use at most 128 MiB of HBM per device.

```python
import math
import jax
import jax.numpy as jnp
import numpy as np
from jax import lax

D = 4096
HEADS = 16
HEAD_DIM = 128
ATT_WIDTH = 2048
GROUP = 64
NBR_LEN = 128
GROUP_DEV = 3
TOKENS = 24576
GROUPS = 384
NB_DEV = 6
NBLOCKS = 768
CAP = 2
N_ENC = 4
N_FSDP = 32


def draw_hidden(key, part):
    key = jax.random.fold_in(key, 1)
    base = jax.random.normal(key, (TOKENS, D), jnp.float32)
    return jnp.clip(base, -60.0, 60.0).astype(jnp.bfloat16)


def draw_neighbour_keys(key, part):
    key = jax.random.fold_in(key, 2)
    base = jax.random.normal(key, (NBLOCKS, NBR_LEN, ATT_WIDTH), jnp.float32)
    return jnp.clip(base, -50.0, 50.0).astype(jnp.bfloat16)


def plant(values, rng, smallest, top_value):
    index_at = [jax.random.randint(jax.random.fold_in(rng, axis), (), 0, length) for axis, length in enumerate(values.shape)]
    longest = values.shape.index(max(values.shape))
    beside = index_at[:longest] + [(index_at[longest] + 1) % values.shape[longest]] + index_at[longest + 1:]
    return values.at[tuple(index_at)].set(smallest).at[tuple(beside)].set(top_value)


def block_levels(stream_key, dims, pieces, least, top_value):
    level, own = 1.0, jax.random.fold_in(stream_key, 6)
    for position, shards_of in pieces:
        draws = jnp.exp(jax.random.uniform(jax.random.fold_in(own, position), (shards_of,), jnp.float32, least / len(pieces), top_value / len(pieces)))
        level = level * jnp.repeat(draws, dims[position] // shards_of).reshape([-1 if axis == position else 1 for axis in range(len(dims))])
    return level


def shared_out(own_key, own, number, rows, count, top, bound, lean):
    sequence = jax.random.permutation(own_key, count)
    heavy_load, ordinary = portions_of(count, rows * top, bound, lean, True), portions_of(count, rows * top, bound, lean, False)
    places = jnp.arange(count)

    def named(sizes, turn):
        used = int((sizes > 0).sum())
        fixed = max(1, used // 4)
        passed = fixed + (places - fixed + turn * (used - fixed)) % max(1, count - fixed)
        return jnp.zeros((count,), jnp.int32).at[sequence[jnp.where(places < fixed, places, passed)]].set(jnp.asarray(sizes, jnp.int32))

    sizes = jnp.where(number % 4 == 0, named(heavy_load, number // 4), named(ordinary, number - number // 4 - 1))
    mixed = jax.random.permutation(jax.random.fold_in(own, 3), count)
    source_of, sink = mixed[0:count // 2 * 2:2], mixed[1:count // 2 * 2:2]
    slack = jnp.minimum(sizes[source_of] - 1, bound - sizes[sink]) // 2
    slack = jnp.where((source_of == sequence[0]) | (sink == sequence[0]) | (sizes[sink] == 0), 0, jnp.maximum(slack, 0))
    passed = jax.random.randint(jax.random.fold_in(own, 4), (count // 2,), 0, 1 << 20) % (slack + 1)
    sizes = sizes.at[source_of].add(-passed).at[sink].add(passed)
    labels = jnp.searchsorted(jnp.cumsum(sizes), jnp.arange(rows * top), side="right").astype(jnp.int32)
    table = labels.reshape(top, rows).T
    table = table[jax.random.permutation(jax.random.fold_in(own, 1), rows)]
    turn = jax.random.randint(jax.random.fold_in(own, 2), (rows, 1), 0, top)
    return jnp.take_along_axis(table, (jnp.arange(top)[None, :] + turn) % top, axis=1)


def portions_of(number_of, total, reach, lean, full):
    portions = [(1 << 20) // math.isqrt(grade ** lean) + 1 for grade in range(1, number_of + 1)]
    largest = reach if full else min(reach, max(-(-total // number_of), total * portions[0] // sum(portions)))
    least = 1 if total - largest >= number_of - 1 else 0
    given, spare = [largest] + [least] * (number_of - 1), total - largest - least * (number_of - 1)
    while spare > 0:
        movable = [i for i in range(1, number_of) if given[i] < largest] or [i for i in range(1, number_of) if given[i] < reach]
        whole, left = sum([portions[i] for i in movable]), spare
        for i in movable:
            extra = min(reach - given[i], max(1, left * portions[i] // whole), spare)
            given[i] = given[i] + extra
            spare = spare - extra
    return np.array(given)


def scatter_about(key, shape, deviation, reach, pieces=(), held_as=jnp.bfloat16):
    drawn = deviation * jax.random.normal(key, shape, jnp.float32)
    if pieces:
        drawn = drawn * block_levels(key, shape, pieces, -0.22, 0.18)
    return jnp.clip(drawn, -reach, reach).astype(held_as)


def setup_inputs(seed: int = 0) -> dict:
    key_of = jax.random.split(jax.random.key(seed), 8)
    hidden = draw_hidden(jax.random.fold_in(key_of[7], 71), 0)
    query_weight = scatter_about(key_of[1], (D, ATT_WIDTH), D ** -0.5, 0.09375, ((0, 32),))
    neighbour_keys = draw_neighbour_keys(jax.random.fold_in(key_of[7], 71), 0)
    neighbour_values = scatter_about(key_of[3], (NBLOCKS, NBR_LEN, ATT_WIDTH), 1.0, 6.0, ((0, 128),))
    neighbour_owner_keys = jax.random.split(jax.random.fold_in(key_of[4], 1), GROUPS // GROUP_DEV)
    neighbour_owner_turns = jax.random.permutation(jax.random.fold_in(key_of[4], 3), GROUPS // GROUP_DEV)
    neighbour_owner = jax.vmap(lambda own, number: shared_out(jax.random.fold_in(key_of[4], 2), own, number, GROUP_DEV, N_ENC, 2, CAP, 2))(neighbour_owner_keys, neighbour_owner_turns).reshape((GROUPS, 2))
    neighbour_row = plant(jax.random.randint(key_of[5], (GROUPS, 2), 0, NB_DEV), jax.random.fold_in(key_of[5], 1), 0, NB_DEV - 1).astype(jnp.int32)
    output_cotangent = scatter_about(key_of[6], (TOKENS, ATT_WIDTH), 1.0, 6.0, ((0, 128),))
    return dict(hidden=hidden, query_weight=query_weight, neighbour_keys=neighbour_keys, neighbour_values=neighbour_values, neighbour_owner=neighbour_owner, neighbour_row=neighbour_row, output_cotangent=output_cotangent)


def to_bfloat(values):
    return lax.optimization_barrier(values.astype(jnp.bfloat16)).astype(jnp.float32)

def partial_attend(query, keys, values):
    score_scale = 1.0 / math.sqrt(HEAD_DIM)
    query_heads = query.astype(jnp.float32).reshape(GROUP, HEADS, HEAD_DIM)
    key_heads = keys.astype(jnp.float32).reshape(NBR_LEN, HEADS, HEAD_DIM)
    value_heads = values.astype(jnp.float32).reshape(NBR_LEN, HEADS, HEAD_DIM)
    scores = jnp.einsum('chd,lhd->hcl', query_heads, key_heads) * score_scale
    peak = lax.optimization_barrier(jnp.max(scores, axis=2))
    exponent = jnp.exp(scores - peak[:, :, None])
    row_total = lax.optimization_barrier(jnp.sum(exponent, axis=2))
    partial_out = jnp.einsum('hcl,lhd->chd', to_bfloat(exponent), value_heads)
    return (partial_out.reshape(GROUP, ATT_WIDTH), peak.T, row_total.T)

def partial_grad(query, keys, values, cotangent, log_total, delta_rows):
    score_scale = 1.0 / math.sqrt(HEAD_DIM)
    query_heads = query.astype(jnp.float32).reshape(GROUP, HEADS, HEAD_DIM)
    key_heads = keys.astype(jnp.float32).reshape(NBR_LEN, HEADS, HEAD_DIM)
    value_heads = values.astype(jnp.float32).reshape(NBR_LEN, HEADS, HEAD_DIM)
    cot_heads = cotangent.astype(jnp.float32).reshape(GROUP, HEADS, HEAD_DIM)
    scores = jnp.einsum('chd,lhd->hcl', query_heads, key_heads) * score_scale
    probs = jnp.exp(scores - log_total.T[:, :, None])
    grad_probs = jnp.einsum('chd,lhd->hcl', cot_heads, value_heads)
    grad_scores = to_bfloat(probs * (grad_probs - delta_rows.T[:, :, None]) * score_scale)
    grad_query = jnp.einsum('hcl,lhd->chd', grad_scores, key_heads).reshape(GROUP, ATT_WIDTH)
    grad_key = jnp.einsum('hcl,chd->lhd', grad_scores, query_heads).reshape(NBR_LEN, ATT_WIDTH)
    grad_value = jnp.einsum('hcl,chd->lhd', to_bfloat(probs), cot_heads).reshape(NBR_LEN, ATT_WIDTH)
    return (grad_query, grad_key.astype(jnp.bfloat16), grad_value.astype(jnp.bfloat16))

def combine(first, second):
    out_a, peak_a, total_a = first
    out_b, peak_b, total_b = second
    peak = jnp.maximum(peak_a, peak_b)
    weight_a = jnp.exp(peak_a - peak)
    weight_b = jnp.exp(peak_b - peak)
    denominator = weight_a * total_a + weight_b * total_b
    leading = out_a.shape[:-1]
    summed = out_a.reshape(leading + (HEADS, HEAD_DIM)) * weight_a[..., None]
    summed = summed + out_b.reshape(leading + (HEADS, HEAD_DIM)) * weight_b[..., None]
    combined = summed / denominator[..., None]
    return (combined.reshape(out_a.shape), peak + jnp.log(denominator))

def row_delta(cotangent, combined):
    leading = combined.shape[:-1]
    product = cotangent.astype(jnp.float32) * combined
    return lax.optimization_barrier(jnp.sum(product.reshape(leading + (HEADS, HEAD_DIM)), axis=-1))

def reference(hidden, query_weight, neighbour_keys, neighbour_values, neighbour_owner, neighbour_row, output_cotangent):
    query = jnp.dot(hidden, query_weight, preferred_element_type=jnp.float32).astype(jnp.bfloat16)
    group_index = jnp.arange(GROUPS, dtype=jnp.int32)
    column = group_index // GROUP_DEV % N_FSDP
    blocks = ((neighbour_owner * N_FSDP + column[:, None]) * NB_DEV + neighbour_row).astype(jnp.int32)
    query_groups = query.reshape(GROUPS, GROUP, ATT_WIDTH)
    cot_groups = output_cotangent.reshape(GROUPS, GROUP, ATT_WIDTH)

    def one_group(inputs):
        group_query, group_cot, group_blocks = inputs
        keys = jnp.take(neighbour_keys, group_blocks, axis=0)
        values = jnp.take(neighbour_values, group_blocks, axis=0)
        first = partial_attend(group_query, keys[0], values[0])
        second = partial_attend(group_query, keys[1], values[1])
        combined, log_total = combine(first, second)
        delta_rows = row_delta(group_cot, combined)
        grads_a = partial_grad(group_query, keys[0], values[0], group_cot, log_total, delta_rows)
        grads_b = partial_grad(group_query, keys[1], values[1], group_cot, log_total, delta_rows)
        grad_query = (grads_a[0] + grads_b[0]).astype(jnp.bfloat16)
        key_terms = jnp.stack([grads_a[1], grads_b[1]])
        value_terms = jnp.stack([grads_a[2], grads_b[2]])
        return (combined.astype(jnp.bfloat16), grad_query, key_terms, value_terms)
    attended, grad_query, key_terms, value_terms = lax.map(one_group, (query_groups, cot_groups, blocks))
    flat_blocks = blocks.reshape(GROUPS * 2)
    grad_keys = jnp.zeros((NBLOCKS, NBR_LEN, ATT_WIDTH), jnp.float32).at[flat_blocks].add(key_terms.reshape(GROUPS * 2, NBR_LEN, ATT_WIDTH).astype(jnp.float32))
    grad_values = jnp.zeros((NBLOCKS, NBR_LEN, ATT_WIDTH), jnp.float32).at[flat_blocks].add(value_terms.reshape(GROUPS * 2, NBR_LEN, ATT_WIDTH).astype(jnp.float32))
    grad_query = grad_query.reshape(TOKENS, ATT_WIDTH)
    grad_hidden = jnp.dot(grad_query, query_weight.T, preferred_element_type=jnp.float32).astype(jnp.bfloat16)
    return (attended.reshape(TOKENS, ATT_WIDTH), grad_hidden, grad_keys.astype(jnp.bfloat16), grad_values.astype(jnp.bfloat16))
```

```python
import functools
import math

import jax
import jax.numpy as jnp
from jax import lax
from jax.experimental import pallas as pl
from jax.experimental.pallas import tpu as pltpu
from jax.sharding import PartitionSpec as P

HEAD = 128
LEN = 128
ROWS = 64
GROUPS = 3
STORED = 6
SLOTS = 8
WIDTH = 2048
SCALE = 1.0 / math.sqrt(HEAD)
F32 = jnp.float32
BF16 = jnp.bfloat16
ANY = pl.BlockSpec(memory_space=pltpu.HBM)
SMEM = pl.BlockSpec(memory_space=pltpu.SMEM)
VMEM = pl.BlockSpec(memory_space=pltpu.VMEM)
CHUNKS = 2
GANG = 8
STEP = 2048


def params(mib):
    return pltpu.CompilerParams(vmem_limit_bytes=mib << 20)


def cost(flops, data, exps=0):
    return pl.CostEstimate(flops=int(flops), bytes_accessed=int(data), transcendentals=int(exps))


def shape(dims, dtype):
    return jax.ShapeDtypeStruct(dims, dtype)


def dot(a, b, ca, cb):
    return lax.dot_general(a, b, (((ca,), (cb,)), ((), ())), preferred_element_type=F32)


def head(h):
    return slice(h * HEAD, (h + 1) * HEAD)


def route_kernel(me, owner, row, pick, want, place, count):
    for k in range(SLOTS):
        pick[k] = 0
        want[k] = -1
    for d in range(4):
        count[d] = 0
    for g in range(GROUPS):
        for j in range(2):
            d = (owner[g, j] - me[0] + 4) % 4
            k = d * 2 + jnp.minimum(count[d], 1)
            count[d] = count[d] + 1
            pick[k] = g
            want[k] = row[g, j]
            place[g * 2 + j] = k


def route(me, owner, row):
    return pl.pallas_call(
        route_kernel,
        out_shape=(shape((SLOTS,), jnp.int32), shape((SLOTS,), jnp.int32), shape((SLOTS,), jnp.int32)),
        in_specs=[SMEM] * 3,
        out_specs=(SMEM, SMEM, SMEM),
        scratch_shapes=[pltpu.SMEM((4,), jnp.int32)],
        name="route",
    )(me, owner, row)


def spread_kernel(pick, cot, *outs):
    for d in range(1, 4):
        for s in range(2):
            outs[d - 1][s] = cot[pick[2 * d + s]]


def spread(pick, cot):
    one = shape((2, ROWS, WIDTH), BF16)
    return pl.pallas_call(
        spread_kernel,
        out_shape=(one,) * 3,
        in_specs=[SMEM, VMEM],
        out_specs=(VMEM,) * 3,
        compiler_params=params(24),
        cost_estimate=cost(1, 20 * ROWS * WIDTH),
        name="spread",
    )(pick, cot)


def query_kernel(steps, pick, hid, w, q, s1, s2, s3, acc):
    i = pl.program_id(0)
    part = dot(hid[...], w[...], 1, 0)

    @pl.when(i == 0)
    def _():
        acc[...] = part

    @pl.when(i > 0)
    def _():
        acc[...] += part

    @pl.when(i == steps - 1)
    def _():
        for g in range(GROUPS):
            q[g] = acc[g * ROWS : (g + 1) * ROWS].astype(BF16)
        for d, out in ((1, s1), (2, s2), (3, s3)):
            for s in range(2):
                out[s] = q[pick[2 * d + s]]


def query(pick, hidden, weights, col, cw):
    depth = hidden.shape[1]
    step = STEP
    steps = depth // step
    c = col // cw
    const = lambda i: (0, 0, 0)
    piece = shape((2, ROWS, cw), BF16)
    return pl.pallas_call(
        functools.partial(query_kernel, steps),
        out_shape=(shape((GROUPS, ROWS, cw), BF16), piece, piece, piece),
        grid=(steps,),
        in_specs=[
            SMEM,
            pl.BlockSpec((GROUPS * ROWS, step), lambda i: (0, i)),
            pl.BlockSpec((step, cw), lambda i: (i, c)),
        ],
        out_specs=(pl.BlockSpec((GROUPS, ROWS, cw), const),) + (pl.BlockSpec((2, ROWS, cw), const),) * 3,
        scratch_shapes=[pltpu.VMEM((GROUPS * ROWS, cw), F32)],
        compiler_params=params(48),
        cost_estimate=cost(2 * 192 * depth * cw, 2 * depth * (192 + cw)),
        name="query",
    )(pick, hidden, weights)


def slot_copies(k, pick, rows, q, c, keys, values, bufs, sems, col, cw):
    d, s = divmod(k, 2)
    cols = pl.ds(col, cw)
    at = pick[k] if d == 0 else s
    row = jnp.maximum(rows[k], 0)
    qb, cb, kb, vb = bufs
    out = [
        pltpu.make_async_copy(q[d].at[at], qb.at[k], sems.at[k, 0]),
        pltpu.make_async_copy(c[d].at[at, :, cols], cb.at[k], sems.at[k, 1]),
    ]
    if keys is not None:
        out += [
            pltpu.make_async_copy(keys.at[row, :, cols], kb.at[k], sems.at[k, 2]),
            pltpu.make_async_copy(values.at[row, :, cols], vb.at[k], sems.at[k, 3]),
        ]
    return out


def wait_slot(k, bufs, sems):
    for n, buf in enumerate(bufs):
        pltpu.make_async_copy(buf.at[k], buf.at[k], sems.at[k, n]).wait()


def rows_of(k, asked):
    d, s = divmod(k, 2)
    return asked[d][2 * d + s]


def fill_rows(asked, rows):
    for k in range(SLOTS):
        rows[k] = rows_of(k, asked)


def forward_kernel(col, cw, *refs):
    pick, asked, refs = refs[0], refs[1:5], refs[5:]
    q, c, keys, values = refs[:4], refs[4:8], refs[8], refs[9]
    p, st = refs[10:14], refs[14:18]
    rows, qb, cb, kb, vb, pb, sb, sems, osems = refs[18:]
    fill_rows(asked, rows)
    bufs = (qb, cb, kb, vb)
    for k in range(SLOTS):
        for one in slot_copies(k, pick, rows, q, c, keys, values, bufs, sems, col, cw):
            one.start()
    lane = lax.broadcasted_iota(jnp.int32, (ROWS, HEAD), 1)
    heads = cw // HEAD

    @pl.loop(0, SLOTS)
    def _(k):
        wait_slot(k, bufs, sems)

        @pl.when(rows[k] >= 0)
        def _():
            stats = jnp.zeros((ROWS, HEAD), F32)
            for base in range(0, heads, GANG):
                span = range(base, base + GANG)
                vals = [vb[k, :, head(h)] for h in span]
                scores = [dot(qb[k, :, head(h)], kb[k, :, head(h)], 1, 1) * SCALE for h in span]
                peaks = [jnp.max(x, axis=1, keepdims=True) for x in scores]
                exps = [jnp.exp(x - m) for x, m in zip(scores, peaks)]
                totals = [jnp.sum(x, axis=1, keepdims=True) for x in exps]
                rounded = [x.astype(BF16) for x in exps]
                parts = [dot(x, v, 1, 0) for x, v in zip(rounded, vals)]
                mixed = [jnp.sum(cb[k, :, head(h)].astype(F32) * x, axis=1, keepdims=True) for h, x in zip(span, parts)]
                for n, h in enumerate(span):
                    stats = jnp.where(lane == h, peaks[n], stats)
                    stats = jnp.where(lane == heads + h, totals[n], stats)
                    stats = jnp.where(lane == 2 * heads + h, mixed[n], stats)
                    pb[k, :, head(h)] = parts[n].astype(BF16)
            sb[k] = stats

    copies = []
    for k in range(SLOTS):
        d, s = divmod(k, 2)
        copies.append(pltpu.make_async_copy(sb.at[k], st[d].at[s], osems.at[k, 0]))
        copies.append(pltpu.make_async_copy(pb.at[k], p[d].at[s], osems.at[k, 1]))
    for one in copies:
        one.start()
    for one in copies:
        one.wait()


def forward(pick, asked, q, c, keys, values, col, cw):
    piece = shape((2, ROWS, cw), BF16)
    small = shape((2, ROWS, HEAD), F32)
    return pl.pallas_call(
        functools.partial(forward_kernel, col, cw),
        out_shape=(piece,) * 4 + (small,) * 4,
        in_specs=[SMEM] * 5 + [ANY] * 10,
        out_specs=(ANY,) * 8,
        scratch_shapes=[
            pltpu.SMEM((SLOTS,), jnp.int32),
            pltpu.VMEM((SLOTS, ROWS, cw), BF16),
            pltpu.VMEM((SLOTS, ROWS, cw), BF16),
            pltpu.VMEM((SLOTS, LEN, cw), BF16),
            pltpu.VMEM((SLOTS, LEN, cw), BF16),
            pltpu.VMEM((SLOTS, ROWS, cw), BF16),
            pltpu.VMEM((SLOTS, ROWS, HEAD), F32),
            pltpu.SemaphoreType.DMA((SLOTS, 4)),
            pltpu.SemaphoreType.DMA((SLOTS, 2)),
        ],
        compiler_params=params(48),
        cost_estimate=cost(SLOTS * 6 * ROWS * LEN * cw, SLOTS * 8 * LEN * cw, SLOTS * ROWS * cw),
        name="forward",
    )(pick, *asked, *q, *c, keys, values)


def backward_kernel(col, cw, *refs):
    pick, asked, refs = refs[0], refs[1:5], refs[5:]
    q, c, keys, values, back = refs[:4], refs[4:8], refs[8], refs[9], refs[10:14]
    gq, gs, pr = refs[14:18], refs[18], refs[19]
    rows, qb, cb, kb, vb, bb, gb, sems, osems = refs[20:]
    fill_rows(asked, rows)
    bufs = (qb, cb, kb, vb, bb)
    for k in range(SLOTS):
        d, s = divmod(k, 2)
        pltpu.make_async_copy(back[d].at[s], bb.at[k], sems.at[k, 4]).start()
        for one in slot_copies(k, pick, rows, q, c, keys, values, bufs[:4], sems, col, cw):
            one.start()
    heads = cw // HEAD

    @pl.loop(0, SLOTS)
    def _(k):
        wait_slot(k, bufs, sems)

        @pl.when(rows[k] >= 0)
        def _():
            stats = bb[k]
            for base in range(0, heads, GANG):
                span = range(base, base + GANG)
                ks = [kb[k, :, head(h)] for h in span]
                scores = [dot(qb[k, :, head(h)], x, 1, 1) * SCALE for h, x in zip(span, ks)]
                grads = [dot(cb[k, :, head(h)], vb[k, :, head(h)], 1, 1) for h in span]
                probs = [jnp.exp(x - stats[:, h : h + 1]) for h, x in zip(span, scores)]
                terms = [
                    (x * (y - stats[:, heads + h : heads + h + 1]) * SCALE).astype(BF16)
                    for h, x, y in zip(span, probs, grads)
                ]
                parts = [dot(x, y, 1, 0) for x, y in zip(terms, ks)]
                for n, h in enumerate(span):
                    pr[k, :, head(h)] = probs[n].astype(BF16)
                    gs[k, :, head(h)] = terms[n]
                    gb[k, :, head(h)] = parts[n].astype(BF16)

    copies = []
    for k in range(SLOTS):
        d, s = divmod(k, 2)
        copies.append(pltpu.make_async_copy(gb.at[k], gq[d].at[s], osems.at[k]))
    for one in copies:
        one.start()
    for one in copies:
        one.wait()


def backward(pick, asked, q, c, keys, values, back, col, cw):
    piece = shape((2, ROWS, cw), BF16)
    every = shape((SLOTS, ROWS, cw), BF16)
    return pl.pallas_call(
        functools.partial(backward_kernel, col, cw),
        out_shape=(piece,) * 4 + (every,) * 2,
        in_specs=[SMEM] * 5 + [ANY] * 14,
        out_specs=(ANY,) * 4 + (VMEM,) * 2,
        scratch_shapes=[
            pltpu.SMEM((SLOTS,), jnp.int32),
            pltpu.VMEM((SLOTS, ROWS, cw), BF16),
            pltpu.VMEM((SLOTS, ROWS, cw), BF16),
            pltpu.VMEM((SLOTS, LEN, cw), BF16),
            pltpu.VMEM((SLOTS, LEN, cw), BF16),
            pltpu.VMEM((SLOTS, ROWS, HEAD), F32),
            pltpu.VMEM((SLOTS, ROWS, cw), BF16),
            pltpu.SemaphoreType.DMA((SLOTS, 5)),
            pltpu.SemaphoreType.DMA((SLOTS,)),
        ],
        compiler_params=params(48),
        cost_estimate=cost(SLOTS * 6 * ROWS * LEN * cw, SLOTS * 8 * LEN * cw, SLOTS * ROWS * cw),
        name="backward",
    )(pick, *asked, *q, *c, keys, values, *back)


def terms_kernel(col, cw, first, *refs):
    pick, asked, refs = refs[0], refs[1:5], refs[5:]
    q, c, gs, pr = refs[:4], refs[4:8], refs[8], refs[9]
    refs = refs[10:] if first else refs[12:]
    dk, dv, rows, qb, cb, ak, av, sems = refs
    fill_rows(asked, rows)
    bufs = (qb, cb)
    for k in range(SLOTS):
        for one in slot_copies(k, pick, rows, q, c, None, None, (qb, cb, None, None), sems, col, cw):
            one.start()
    ak[...] = jnp.zeros_like(ak)
    av[...] = jnp.zeros_like(av)

    @pl.loop(0, SLOTS)
    def _(k):
        wait_slot(k, bufs, sems)

        @pl.when(rows[k] >= 0)
        def _():
            row = jnp.maximum(rows[k], 0)
            for h in range(cw // HEAD):
                kt = dot(gs[k, :, head(h)], qb[k, :, head(h)], 0, 0)
                vt = dot(pr[k, :, head(h)], cb[k, :, head(h)], 0, 0)
                ak[row, :, head(h)] += kt.astype(BF16).astype(F32)
                av[row, :, head(h)] += vt.astype(BF16).astype(F32)

    dk[...] = ak[...].astype(BF16)
    dv[...] = av[...].astype(BF16)


def terms(pick, asked, q, c, gs, pr, before, col, cw):
    whole = shape((STORED, LEN, WIDTH), BF16)
    out = pl.BlockSpec((STORED, LEN, cw), lambda i: (0, 0, col // cw))
    first = before is None
    args = (pick, *asked, *q, *c, gs, pr) + (() if first else before)
    return pl.pallas_call(
        functools.partial(terms_kernel, col, cw, first),
        out_shape=(whole,) * 2,
        grid=(1,),
        in_specs=[SMEM] * 5 + [ANY] * 8 + [VMEM] * 2 + ([] if first else [ANY] * 2),
        out_specs=(out,) * 2,
        scratch_shapes=[
            pltpu.SMEM((SLOTS,), jnp.int32),
            pltpu.VMEM((SLOTS, ROWS, cw), BF16),
            pltpu.VMEM((SLOTS, ROWS, cw), BF16),
            pltpu.VMEM((STORED, LEN, cw), F32),
            pltpu.VMEM((STORED, LEN, cw), F32),
            pltpu.SemaphoreType.DMA((SLOTS, 2)),
        ],
        input_output_aliases={} if first else {15: 0, 16: 1},
        compiler_params=params(56),
        cost_estimate=cost(SLOTS * 4 * ROWS * LEN * cw, SLOTS * 8 * ROWS * cw + 24 * LEN * cw),
        name="terms",
    )(*args)


def settle_kernel(heads, pick, place, s0, s1, s2, s3, b0, b1, b2, b3, weight, sb, res):
    for d, ref in enumerate((s0, s1, s2, s3)):
        for s in range(2):
            sb[2 * d + s] = ref[s]
    lane = lax.broadcasted_iota(jnp.int32, (ROWS, HEAD), 1)
    for g in range(GROUPS):
        x, y = sb[place[2 * g]], sb[place[2 * g + 1]]
        move = lambda a, n: pltpu.roll(a, (HEAD - n * heads) % HEAD, 1)
        keep = lane < heads
        px, py = jnp.where(keep, x, 0.0), jnp.where(keep, y, 0.0)
        tx = jnp.where(keep, move(x, 1), 1.0)
        ty = jnp.where(keep, move(y, 1), 1.0)
        mx = jnp.where(keep, move(x, 2), 0.0)
        my = jnp.where(keep, move(y, 2), 0.0)
        top = jnp.maximum(px, py)
        ax, ay = jnp.exp(px - top), jnp.exp(py - top)
        total = ax * tx + ay * ty
        log_total = top + jnp.log(total)
        delta = (ax * mx + ay * my) / total
        res[g] = jnp.where(keep, log_total, pltpu.roll(delta, heads, 1))
        weight[g] = jnp.where(keep, ax / total, pltpu.roll(ay / total, heads, 1))
    for d, ref in enumerate((b0, b1, b2, b3)):
        for s in range(2):
            ref[s] = res[pick[2 * d + s]]


def settle(pick, place, stats, heads):
    small = shape((2, ROWS, HEAD), F32)
    return pl.pallas_call(
        functools.partial(settle_kernel, heads),
        out_shape=(small,) * 4 + (shape((GROUPS, ROWS, HEAD), F32),),
        in_specs=[SMEM] * 2 + [VMEM] * 4,
        out_specs=(VMEM,) * 5,
        scratch_shapes=[pltpu.VMEM((SLOTS, ROWS, HEAD), F32), pltpu.VMEM((GROUPS, ROWS, HEAD), F32)],
        cost_estimate=cost(1e5, 1e6, 1e5),
        name="settle",
    )(pick, place, *stats)


def attend_kernel(heads, first, place, p0, p1, p2, p3, weight, *refs):
    out, pb = refs if first else refs[1:]
    for d, ref in enumerate((p0, p1, p2, p3)):
        for s in range(2):
            pb[2 * d + s] = ref[s]
    for g in range(GROUPS):
        a, b = place[2 * g], place[2 * g + 1]
        w = weight[g]
        for h in range(heads):
            x = pb[a, :, head(h)].astype(F32) * w[:, h : h + 1]
            y = pb[b, :, head(h)].astype(F32) * w[:, heads + h : heads + h + 1]
            out[g * ROWS : (g + 1) * ROWS, head(h)] = (x + y).astype(BF16)


def attend(place, p, weight, before, col, cw):
    first = before is None
    return pl.pallas_call(
        functools.partial(attend_kernel, cw // HEAD, first),
        out_shape=shape((GROUPS * ROWS, WIDTH), BF16),
        grid=(1,),
        in_specs=[SMEM] + [VMEM] * 5 + ([] if first else [ANY]),
        out_specs=pl.BlockSpec((GROUPS * ROWS, cw), lambda i: (0, col // cw)),
        scratch_shapes=[pltpu.VMEM((SLOTS, ROWS, cw), BF16)],
        input_output_aliases={} if first else {6: 0},
        compiler_params=params(32),
        cost_estimate=cost(1e6, 12 * ROWS * cw * 2),
        name="attend",
    )(place, *p, weight, *(() if first else (before,)))


def grad_kernel(first, last, place, g0, g1, g2, g3, w, *refs):
    before, refs = (None, refs) if first else (refs[0], refs[1:])
    out, gb, gq, sems = refs

    @pl.when(pl.program_id(0) == 0)
    def _():
        copies = []
        for d, ref in enumerate((g0, g1, g2, g3)):
            copies.append(pltpu.make_async_copy(ref, gb.at[pl.ds(2 * d, 2)], sems.at[d]))
        for one in copies:
            one.start()
        for one in copies:
            one.wait()
        for g in range(GROUPS):
            both = gb[place[2 * g]].astype(F32) + gb[place[2 * g + 1]].astype(F32)
            gq[g * ROWS : (g + 1) * ROWS] = both.astype(BF16)

    part = dot(gq[...], w[...], 1, 1)
    if not first:
        part = part + before[...]
    out[...] = part.astype(out.dtype)


def grad(place, g, weights, before, last, col, cw):
    depth = weights.shape[0]
    step = STEP
    first = before is None
    block = pl.BlockSpec((GROUPS * ROWS, step), lambda i: (0, i))
    return pl.pallas_call(
        functools.partial(grad_kernel, first, last),
        out_shape=shape((GROUPS * ROWS, depth), BF16 if last else F32),
        grid=(depth // step,),
        in_specs=[SMEM] + [ANY] * 4 + [pl.BlockSpec((step, cw), lambda i: (i, col // cw))] + ([] if first else [block]),
        out_specs=block,
        scratch_shapes=[
            pltpu.VMEM((SLOTS, ROWS, cw), BF16),
            pltpu.VMEM((GROUPS * ROWS, cw), BF16),
            pltpu.SemaphoreType.DMA((4,)),
        ],
        compiler_params=params(48),
        cost_estimate=cost(2 * 192 * depth * cw, 2 * depth * (384 + cw)),
        name="grad",
    )(place, *g, weights, *(() if first else (before,)))


def shift(x, d):
    return lax.ppermute(x, "enc", [(i, (i + d) % 4) for i in range(4)])


def to_owner(pieces):
    return [shift(x, d + 1) for d, x in enumerate(pieces)]


def to_home(pieces):
    return [shift(x, -(d + 1)) for d, x in enumerate(pieces)]


def per_device(hidden, query_weight, keys, values, owner, row, cotangent):
    me = lax.axis_index("enc").astype(jnp.int32).reshape(1)
    pick, want, place = route(me, owner, row)
    asked = [want] + to_owner([want] * 3)
    cot = cotangent.reshape(GROUPS, ROWS, WIDTH)
    c = [cot] + to_owner(spread(pick, cot))
    weights = lax.all_gather(query_weight, "fsdp", axis=0, tiled=True)
    cw = WIDTH // CHUNKS
    cols = [i * cw for i in range(CHUNKS)]
    qs, gqs, ps, scales = [], [], [], []
    for col in cols:
        q, *sends = query(pick, hidden, weights, col, cw)
        qs.append([q] + to_owner(sends))
    stats = []
    for col, q in zip(cols, qs):
        out = forward(pick, asked, q, c, keys, values, col, cw)
        ps.append([out[0]] + to_home(out[1:4]))
        stats.append([out[4]] + to_home(out[5:8]))
    grads, attended = None, None
    backs = []
    for col, q, st in zip(cols, qs, stats):
        *back, weight = settle(pick, place, st, cw // HEAD)
        backs.append([back[0]] + to_owner(back[1:4]))
        scales.append(weight)
    for col, q, back in zip(cols, qs, backs):
        out = backward(pick, asked, q, c, keys, values, back, col, cw)
        gqs.append([out[0]] + to_home(out[1:4]))
        grads = terms(pick, asked, q, c, out[4], out[5], grads, col, cw)
    for col, p, weight in zip(cols, ps, scales):
        attended = attend(place, p, weight, attended, col, cw)
    total = None
    for col, g in zip(cols, gqs):
        total = grad(place, g, weights, total, col == cols[-1], col, cw)
    return attended, total, grads[0], grads[1]


def solution(mesh):
    rows = P(("enc", "fsdp"), None)
    blocks = P(("enc", "fsdp"), None, None)
    return jax.shard_map(
        per_device,
        mesh=mesh,
        in_specs=(rows, P("fsdp", None), blocks, blocks, rows, rows, rows),
        out_specs=(rows, rows, blocks, blocks),
        check_vma=False,
    )
```

```python
import functools
import math

import jax
import jax.numpy as jnp
from jax import lax
from jax.experimental import pallas as pl
from jax.experimental.pallas import tpu as pltpu
from jax.sharding import PartitionSpec as P

HEAD = 128
LEN = 128
ROWS = 64
GROUPS = 3
STORED = 6
SLOTS = 8
WIDTH = 2048
SCALE = 1.0 / math.sqrt(HEAD)
F32 = jnp.float32
BF16 = jnp.bfloat16
ANY = pl.BlockSpec(memory_space=pltpu.HBM)
SMEM = pl.BlockSpec(memory_space=pltpu.SMEM)
VMEM = pl.BlockSpec(memory_space=pltpu.VMEM)


def whole(*dims):
    return pl.BlockSpec(dims, lambda i: (0,) * len(dims))


GANG = 8
HOME_GANG = 4
HEADS = 16
BIG = 58
STEP = 1024
GSTEP = 1024


def params(mib):
    return pltpu.CompilerParams(vmem_limit_bytes=mib << 20)


def cost(flops, data, exps=0):
    return pl.CostEstimate(flops=int(flops), bytes_accessed=int(data), transcendentals=int(exps))


def shape(dims, dtype):
    return jax.ShapeDtypeStruct(dims, dtype)


def dot(a, b, ca, cb):
    return lax.dot_general(a, b, (((ca,), (cb,)), ((), ())), preferred_element_type=F32)


def head(h):
    return slice(h * HEAD, (h + 1) * HEAD)


def route_kernel(me, owner, row, pick, want, place, count):
    for k in range(SLOTS):
        pick[k] = 0
        want[k] = -1
    for d in range(4):
        count[d] = 0
    for g in range(GROUPS):
        for j in range(2):
            d = (owner[g, j] - me[0] + 4) % 4
            k = d * 2 + jnp.minimum(count[d], 1)
            count[d] = count[d] + 1
            pick[k] = g
            want[k] = row[g, j]
            place[g * 2 + j] = k


def route(me, owner, row):
    return pl.pallas_call(
        route_kernel,
        out_shape=(shape((SLOTS,), jnp.int32), shape((SLOTS,), jnp.int32), shape((SLOTS,), jnp.int32)),
        in_specs=[SMEM] * 3,
        out_specs=(SMEM, SMEM, SMEM),
        scratch_shapes=[pltpu.SMEM((4,), jnp.int32)],
        name="route",
    )(me, owner, row)


def spread_kernel(pick, cot, *outs):
    for d in range(1, 4):
        for s in range(2):
            outs[d - 1][s] = cot[pick[2 * d + s]]


def spread(pick, cot):
    one = shape((2, ROWS, WIDTH), BF16)
    return pl.pallas_call(
        spread_kernel,
        out_shape=(one,) * 3,
        grid=(1,),
        in_specs=[SMEM, whole(GROUPS, ROWS, WIDTH)],
        out_specs=(whole(2, ROWS, WIDTH),) * 3,
        compiler_params=params(BIG),
        cost_estimate=cost(1, 20 * ROWS * WIDTH),
        name="spread",
    )(pick, cot)


def query_kernel(steps, pick, hid, w, q, s1, s2, s3, acc):
    i = pl.program_id(0)
    part = dot(hid[...], w[...], 1, 0)

    @pl.when(i == 0)
    def _():
        acc[...] = part

    @pl.when(i > 0)
    def _():
        acc[...] += part

    @pl.when(i == steps - 1)
    def _():
        for g in range(GROUPS):
            q[g] = acc[g * ROWS : (g + 1) * ROWS].astype(BF16)
        for d, out in ((1, s1), (2, s2), (3, s3)):
            for s in range(2):
                out[s] = q[pick[2 * d + s]]


def query(pick, hidden, weights, col, cw):
    depth = hidden.shape[1]
    step = STEP
    steps = depth // step
    c = col // cw
    const = lambda i: (0, 0, 0)
    piece = shape((2, ROWS, cw), BF16)
    return pl.pallas_call(
        functools.partial(query_kernel, steps),
        out_shape=(shape((GROUPS, ROWS, cw), BF16), piece, piece, piece),
        grid=(steps,),
        in_specs=[
            SMEM,
            pl.BlockSpec((GROUPS * ROWS, step), lambda i: (0, i)),
            pl.BlockSpec((step, cw), lambda i: (i, c)),
        ],
        out_specs=(pl.BlockSpec((GROUPS, ROWS, cw), const),) + (pl.BlockSpec((2, ROWS, cw), const),) * 3,
        scratch_shapes=[pltpu.VMEM((GROUPS * ROWS, cw), F32)],
        compiler_params=params(BIG),
        cost_estimate=cost(2 * 192 * depth * cw, 2 * depth * (192 + cw)),
        name="query",
    )(pick, hidden, weights)


def rows_of(k, asked):
    d, s = divmod(k, 2)
    return asked[d][2 * d + s]


def fill_rows(asked, rows):
    for k in range(SLOTS):
        rows[k] = rows_of(k, asked)


def wait_slot(k, bufs, sems):
    for n, buf in enumerate(bufs):
        pltpu.make_async_copy(buf.at[k], buf.at[k], sems.at[k, n]).wait()


def collect_kernel(*refs):
    asked, table, outs, buf, sems, osems = refs[:4], refs[4], refs[5:8], refs[8], refs[9], refs[10]
    loads, stores = [], []
    for k in range(2, SLOTS):
        d, s = divmod(k, 2)
        row = jnp.maximum(rows_of(k, asked), 0)
        loads.append(pltpu.make_async_copy(table.at[row], buf.at[k - 2], sems.at[k - 2]))
        stores.append(pltpu.make_async_copy(buf.at[k - 2], outs[d - 1].at[s], osems.at[k - 2]))
    for one in loads:
        one.start()
    for one, two in zip(loads, stores):
        one.wait()
        two.start()
    for one in stores:
        one.wait()


def collect(asked, table):
    one = shape((2, LEN, WIDTH), BF16)
    return pl.pallas_call(
        collect_kernel,
        out_shape=(one,) * 3,
        in_specs=[SMEM] * 4 + [ANY],
        out_specs=(ANY,) * 3,
        scratch_shapes=[
            pltpu.VMEM((SLOTS - 2, LEN, WIDTH), BF16),
            pltpu.SemaphoreType.DMA((SLOTS - 2,)),
            pltpu.SemaphoreType.DMA((SLOTS - 2,)),
        ],
        compiler_params=params(BIG),
        cost_estimate=cost(1, 24 * LEN * WIDTH),
        name="collect",
    )(*asked, table)


def home_kernel(*refs):
    pick, place, want, q, c, keys, values = refs[:7]
    ks, vs = (keys,) + refs[7:10], (values,) + refs[10:13]
    att, gq, backs = refs[13], refs[14], refs[15:19]
    qb, cb, kb, vb, res, sems, gsems = refs[19:]
    for g in range(GROUPS):
        pltpu.make_async_copy(q.at[g], qb.at[g], gsems.at[g, 0]).start()
        pltpu.make_async_copy(c.at[g], cb.at[g], gsems.at[g, 1]).start()
        for r in (2 * g, 2 * g + 1):
            at = place[r]
            for d in range(4):

                @pl.when(at // 2 == d)
                def _(r=r, d=d, at=at):
                    s = jnp.maximum(want[at], 0) if d == 0 else at - 2 * d
                    pltpu.make_async_copy(ks[d].at[s], kb.at[r], sems.at[r, 0]).start()
                    pltpu.make_async_copy(vs[d].at[s], vb.at[r], sems.at[r, 1]).start()

    lane = lax.broadcasted_iota(jnp.int32, (ROWS, HEAD), 1)

    @pl.loop(0, GROUPS)
    def _(g):
        wait_slot(g, (qb, cb), gsems)
        for j in range(2):
            wait_slot(2 * g + j, (kb, vb), sems)
        stats = jnp.zeros((ROWS, HEAD), F32)
        out = pl.ds(pl.multiple_of(g * ROWS, ROWS), ROWS)
        for base in range(0, HEADS, HOME_GANG):
            span = [(h, j) for h in range(base, base + HOME_GANG) for j in range(2)]
            key = {(h, j): kb[2 * g + j, :, head(h)] for h, j in span}
            value = {(h, j): vb[2 * g + j, :, head(h)] for h, j in span}
            score = {(h, j): dot(qb[g, :, head(h)], key[h, j], 1, 1) * SCALE for h, j in span}
            slope = {(h, j): dot(cb[g, :, head(h)], value[h, j], 1, 1) for h, j in span}
            peak = {x: jnp.max(score[x], axis=1, keepdims=True) for x in span}
            e = {x: jnp.exp(score[x] - peak[x]) for x in span}
            total = {x: jnp.sum(e[x], axis=1, keepdims=True) for x in span}
            part = {x: dot(e[x].astype(BF16), value[x], 1, 0) for x in span}
            for h in range(base, base + HOME_GANG):
                top = jnp.maximum(peak[h, 0], peak[h, 1])
                scale = [jnp.exp(peak[h, j] - top) for j in range(2)]
                below = scale[0] * total[h, 0] + scale[1] * total[h, 1]
                scale = [x / below for x in scale]
                mix = part[h, 0] * scale[0] + part[h, 1] * scale[1]
                att[out, head(h)] = mix.astype(BF16)
                delta = jnp.sum(cb[g, :, head(h)].astype(F32) * mix, axis=1, keepdims=True)
                stats = jnp.where(lane == h, top + jnp.log(below), stats)
                stats = jnp.where(lane == HEADS + h, delta, stats)
                both = None
                for j in range(2):
                    gs = (e[h, j] * scale[j] * (slope[h, j] - delta) * SCALE).astype(BF16)
                    one = dot(gs, key[h, j], 1, 0)
                    both = one if both is None else both + one
                gq[out, head(h)] = both.astype(BF16)
        res[g] = stats

    for d in range(4):
        for s in range(2):
            backs[d][s] = res[pick[2 * d + s]]


def home(pick, place, want, q, c, keys, values, ks, vs):
    rows = shape((GROUPS * ROWS, WIDTH), BF16)
    small = shape((2, ROWS, HEAD), F32)
    return pl.pallas_call(
        home_kernel,
        out_shape=(rows,) * 2 + (small,) * 4,
        grid=(1,),
        in_specs=[SMEM] * 3 + [ANY] * 10,
        out_specs=(whole(GROUPS * ROWS, WIDTH),) * 2 + (whole(2, ROWS, HEAD),) * 4,
        scratch_shapes=[
            pltpu.VMEM((GROUPS, ROWS, WIDTH), BF16),
            pltpu.VMEM((GROUPS, ROWS, WIDTH), BF16),
            pltpu.VMEM((2 * GROUPS, LEN, WIDTH), BF16),
            pltpu.VMEM((2 * GROUPS, LEN, WIDTH), BF16),
            pltpu.VMEM((GROUPS, ROWS, HEAD), F32),
            pltpu.SemaphoreType.DMA((2 * GROUPS, 2)),
            pltpu.SemaphoreType.DMA((GROUPS, 2)),
        ],
        compiler_params=params(BIG),
        cost_estimate=cost(6 * 8 * ROWS * LEN * WIDTH, 30 * LEN * WIDTH, 6 * ROWS * WIDTH),
        name="home",
    )(pick, place, want, q, c, keys, values, *ks, *vs)


def terms_kernel(*refs):
    pick, asked, refs = refs[0], refs[1:5], refs[5:]
    q, c, keys, values, back = refs[:4], refs[4:8], refs[8], refs[9], refs[10:14]
    dk, dv, rows, seen, qb, cb, kb, vb, bb, sems = refs[14:]
    fill_rows(asked, rows)
    bufs = (qb, cb, kb, vb, bb)
    for b in range(STORED):
        seen[b] = 0
    for k in range(SLOTS):
        d, s = divmod(k, 2)
        at = pick[k] if d == 0 else s
        row = jnp.maximum(rows[k], 0)
        pltpu.make_async_copy(q[d].at[at], qb.at[k], sems.at[k, 0]).start()
        pltpu.make_async_copy(c[d].at[at], cb.at[k], sems.at[k, 1]).start()
        pltpu.make_async_copy(keys.at[row], kb.at[k], sems.at[k, 2]).start()
        pltpu.make_async_copy(values.at[row], vb.at[k], sems.at[k, 3]).start()
        pltpu.make_async_copy(back[d].at[s], bb.at[k], sems.at[k, 4]).start()

    def one_slot(k, row, add):
        stats = bb[k]
        for base in range(0, HEADS, GANG):
            span = range(base, base + GANG)
            scores = [dot(qb[k, :, head(h)], kb[k, :, head(h)], 1, 1) * SCALE for h in span]
            slopes = [dot(cb[k, :, head(h)], vb[k, :, head(h)], 1, 1) for h in span]
            probs = [jnp.exp(x - stats[:, h : h + 1]) for h, x in zip(span, scores)]
            gs = [
                (x * (y - stats[:, HEADS + h : HEADS + h + 1]) * SCALE).astype(BF16)
                for h, x, y in zip(span, probs, slopes)
            ]
            kts = [dot(x, qb[k, :, head(h)], 0, 0) for h, x in zip(span, gs)]
            vts = [dot(x.astype(BF16), cb[k, :, head(h)], 0, 0) for h, x in zip(span, probs)]
            for h, kt, vt in zip(span, kts, vts):
                if add:
                    kt = kt.astype(BF16).astype(F32) + dk[row, :, head(h)].astype(F32)
                    vt = vt.astype(BF16).astype(F32) + dv[row, :, head(h)].astype(F32)
                dk[row, :, head(h)] = kt.astype(BF16)
                dv[row, :, head(h)] = vt.astype(BF16)

    @pl.loop(0, SLOTS)
    def _(k):
        wait_slot(k, bufs, sems)
        row = jnp.maximum(rows[k], 0)
        valid = rows[k] >= 0

        @pl.when(valid & (seen[row] == 0))
        def _():
            one_slot(k, row, False)

        @pl.when(valid & (seen[row] > 0))
        def _():
            one_slot(k, row, True)

        seen[row] = seen[row] + valid.astype(jnp.int32)

    for b in range(STORED):

        @pl.when(seen[b] == 0)
        def _(b=b):
            dk[b] = jnp.zeros((LEN, WIDTH), BF16)
            dv[b] = jnp.zeros((LEN, WIDTH), BF16)


def terms(pick, asked, q, c, keys, values, back):
    full = shape((STORED, LEN, WIDTH), BF16)
    return pl.pallas_call(
        terms_kernel,
        out_shape=(full,) * 2,
        grid=(1,),
        in_specs=[SMEM] * 5 + [ANY] * 14,
        out_specs=(whole(STORED, LEN, WIDTH),) * 2,
        scratch_shapes=[
            pltpu.SMEM((SLOTS,), jnp.int32),
            pltpu.SMEM((STORED,), jnp.int32),
            pltpu.VMEM((SLOTS, ROWS, WIDTH), BF16),
            pltpu.VMEM((SLOTS, ROWS, WIDTH), BF16),
            pltpu.VMEM((SLOTS, LEN, WIDTH), BF16),
            pltpu.VMEM((SLOTS, LEN, WIDTH), BF16),
            pltpu.VMEM((SLOTS, ROWS, HEAD), F32),
            pltpu.SemaphoreType.DMA((SLOTS, 5)),
        ],
        compiler_params=params(BIG),
        cost_estimate=cost(SLOTS * 8 * ROWS * LEN * WIDTH, 44 * LEN * WIDTH, SLOTS * ROWS * WIDTH),
        name="terms",
    )(pick, *asked, *q, *c, keys, values, *back)


def grad_kernel(gq, w, out):
    out[...] = dot(gq[...], w[...], 1, 1).astype(BF16)


def grad(gq, weights):
    depth, step = weights.shape[0], GSTEP
    return pl.pallas_call(
        grad_kernel,
        out_shape=shape((GROUPS * ROWS, depth), BF16),
        grid=(depth // step,),
        in_specs=[whole(GROUPS * ROWS, WIDTH), pl.BlockSpec((step, WIDTH), lambda i: (i, 0))],
        out_specs=pl.BlockSpec((GROUPS * ROWS, step), lambda i: (0, i)),
        compiler_params=params(BIG),
        cost_estimate=cost(2 * 192 * depth * WIDTH, 2 * depth * (192 + WIDTH)),
        name="grad",
    )(gq, weights)


def shift(x, d):
    return lax.ppermute(x, "enc", [(i, (i + d) % 4) for i in range(4)])


def to_owner(pieces):
    return [shift(x, d + 1) for d, x in enumerate(pieces)]


def to_home(pieces):
    return [shift(x, -(d + 1)) for d, x in enumerate(pieces)]


def per_device(hidden, query_weight, keys, values, owner, row, cotangent):
    me = lax.axis_index("enc").astype(jnp.int32).reshape(1)
    weights = lax.all_gather(query_weight, "fsdp", axis=0, tiled=True)
    pick, want, place = route(me, owner, row)
    asked = [want] + to_owner([want] * 3)
    ks = to_home(collect(asked, keys))
    vs = to_home(collect(asked, values))
    cot = cotangent.reshape(GROUPS, ROWS, WIDTH)
    c = [cot] + to_owner(spread(pick, cot))
    q, *sends = query(pick, hidden, weights, 0, WIDTH)
    qs = [q] + to_owner(sends)
    attended, gq, *back = home(pick, place, want, q, cot, keys, values, ks, vs)
    back = [back[0]] + to_owner(back[1:])
    grad_hidden = grad(gq, weights)
    grad_keys, grad_values = terms(pick, asked, qs, c, keys, values, back)
    return attended, grad_hidden, grad_keys, grad_values


def solution(mesh):
    rows = P(("enc", "fsdp"), None)
    blocks = P(("enc", "fsdp"), None, None)
    return jax.shard_map(
        per_device,
        mesh=mesh,
        in_specs=(rows, P("fsdp", None), blocks, blocks, rows, rows, rows),
        out_specs=(rows, rows, blocks, blocks),
        check_vma=False,
    )
```

```python
import functools
import math

import jax
import jax.numpy as jnp
from jax import lax
from jax.experimental import pallas as pl
from jax.experimental.pallas import tpu as pltpu
from jax.sharding import PartitionSpec as P

HEAD = 128
LEN = 128
ROWS = 64
GROUPS = 3
STORED = 6
SLOTS = 8
WIDTH = 2048
SCALE = 1.0 / math.sqrt(HEAD)
F32 = jnp.float32
BF16 = jnp.bfloat16
ANY = pl.BlockSpec(memory_space=pltpu.HBM)
SMEM = pl.BlockSpec(memory_space=pltpu.SMEM)
VMEM = pl.BlockSpec(memory_space=pltpu.VMEM)


def whole(*dims):
    return pl.BlockSpec(dims, lambda i: (0,) * len(dims))


TWIDTH = 1024
GANG = 8
HOME_GANG = 4
PARTS = ((0, 1536), (1536, 512))
HEADS = 16
BIG = 58
QSTEP = 512
GSTEP = 1024


def params(mib):
    return pltpu.CompilerParams(vmem_limit_bytes=mib << 20)


def cost(flops, data, exps=0):
    return pl.CostEstimate(flops=int(flops), bytes_accessed=int(data), transcendentals=int(exps))


def shape(dims, dtype):
    return jax.ShapeDtypeStruct(dims, dtype)


def dot(a, b, ca, cb):
    return lax.dot_general(a, b, (((ca,), (cb,)), ((), ())), preferred_element_type=F32)


def head(h):
    return slice(h * HEAD, (h + 1) * HEAD)


def route_kernel(me, table, pick, want, place, count):
    for k in range(SLOTS):
        pick[k] = 0
        want[k] = -1
    for d in range(4):
        count[d] = 0
    for g in range(GROUPS):
        for j in range(2):
            d = (table[g, j] - me[0] + 4) % 4
            k = d * 2 + jnp.minimum(count[d], 1)
            count[d] = count[d] + 1
            pick[k] = g
            want[k] = table[g, 2 + j]
            place[g * 2 + j] = k


def route(me, table):
    return pl.pallas_call(
        route_kernel,
        out_shape=(shape((SLOTS,), jnp.int32), shape((SLOTS,), jnp.int32), shape((SLOTS,), jnp.int32)),
        in_specs=[SMEM] * 2,
        out_specs=(SMEM, SMEM, SMEM),
        scratch_shapes=[pltpu.SMEM((4,), jnp.int32)],
        name="route",
    )(me, table)


def spread_kernel(pick, cot, *outs):
    for d in range(1, 4):
        for s in range(2):
            outs[d - 1][s] = cot[pick[2 * d + s]]


def spread(pick, cot):
    one = shape((2, ROWS, WIDTH), BF16)
    return pl.pallas_call(
        spread_kernel,
        out_shape=(one,) * 3,
        grid=(1,),
        in_specs=[SMEM, whole(GROUPS, ROWS, WIDTH)],
        out_specs=(whole(2, ROWS, WIDTH),) * 3,
        compiler_params=params(BIG),
        cost_estimate=cost(1, 20 * ROWS * WIDTH),
        name="spread",
    )(pick, cot)


def query_kernel(pick, hid, w, q, s1, s2, s3):
    part = dot(hid[...], w[...], 1, 0)
    for g in range(GROUPS):
        q[g] = part[g * ROWS : (g + 1) * ROWS].astype(BF16)
    for d, out in ((1, s1), (2, s2), (3, s3)):
        for s in range(2):
            out[s] = q[pick[2 * d + s]]


def query(pick, hidden, weights):
    depth = hidden.shape[1]
    piece = shape((2, ROWS, WIDTH), BF16)
    block = pl.BlockSpec((2, ROWS, QSTEP), lambda i: (0, 0, i))
    return pl.pallas_call(
        query_kernel,
        out_shape=(shape((GROUPS, ROWS, WIDTH), BF16), piece, piece, piece),
        grid=(WIDTH // QSTEP,),
        in_specs=[
            SMEM,
            whole(GROUPS * ROWS, depth),
            pl.BlockSpec((depth, QSTEP), lambda i: (0, i)),
        ],
        out_specs=(pl.BlockSpec((GROUPS, ROWS, QSTEP), lambda i: (0, 0, i)), block, block, block),
        compiler_params=params(BIG),
        cost_estimate=cost(2 * 192 * depth * WIDTH, 2 * depth * (192 + WIDTH)),
        name="query",
    )(pick, hidden, weights)


def rows_of(k, asked):
    d, s = divmod(k, 2)
    return asked[d][2 * d + s]


def fill_rows(asked, rows):
    for k in range(SLOTS):
        rows[k] = rows_of(k, asked)


def wait_slot(k, bufs, sems):
    for n, buf in enumerate(bufs):
        pltpu.make_async_copy(buf.at[k], buf.at[k], sems.at[k, n]).wait()


def collect_kernel(col, cw, *refs):
    asked, tables, outs, buf, sems, osems = refs[:4], refs[4:6], refs[6:9], refs[9], refs[10], refs[11]
    loads, stores = [], []
    for k in range(2, SLOTS):
        d, s = divmod(k, 2)
        row = jnp.maximum(rows_of(k, asked), 0)
        for n in range(2):
            here = buf.at[k - 2, n]
            loads.append(pltpu.make_async_copy(tables[n].at[row, :, pl.ds(col, cw)], here, sems.at[k - 2, n]))
            stores.append(pltpu.make_async_copy(here, outs[d - 1].at[s, n], osems.at[k - 2, n]))
    for one in loads:
        one.start()
    for one, two in zip(loads, stores):
        one.wait()
        two.start()
    for one in stores:
        one.wait()


def collect(asked, keys, values, col, cw):
    one = shape((2, 2, LEN, cw), BF16)
    return pl.pallas_call(
        functools.partial(collect_kernel, col, cw),
        out_shape=(one,) * 3,
        in_specs=[SMEM] * 4 + [ANY] * 2,
        out_specs=(ANY,) * 3,
        scratch_shapes=[
            pltpu.VMEM((SLOTS - 2, 2, LEN, cw), BF16),
            pltpu.SemaphoreType.DMA((SLOTS - 2, 2)),
            pltpu.SemaphoreType.DMA((SLOTS - 2, 2)),
        ],
        compiler_params=params(BIG),
        cost_estimate=cost(1, 48 * LEN * cw),
        name="collect",
    )(*asked, keys, values)


def home_kernel(col, cw, first, last, *refs):
    pick, place, want, q, c, keys, values = refs[:7]
    pairs, refs = refs[7:10], refs[10:]
    if not first:
        before, refs = refs[0], refs[2:]
    att, gq, refs = refs[0], refs[1], refs[2:]
    if last:
        backs, refs = refs[:4], refs[4:]
    qb, cb, kb, vb, res, sems, gsems = refs
    cols = pl.ds(col, cw)
    for g in range(GROUPS):
        pltpu.make_async_copy(q.at[g, :, cols], qb.at[g], gsems.at[g, 0]).start()
        pltpu.make_async_copy(c.at[g, :, cols], cb.at[g], gsems.at[g, 1]).start()
        for r in (2 * g, 2 * g + 1):
            at = place[r]
            for d in range(4):

                @pl.when(at // 2 == d)
                def _(r=r, d=d, at=at):
                    if d == 0:
                        s = jnp.maximum(want[at], 0)
                        ends = keys.at[s, :, cols], values.at[s, :, cols]
                    else:
                        ends = pairs[d - 1].at[at - 2 * d, 0], pairs[d - 1].at[at - 2 * d, 1]
                    pltpu.make_async_copy(ends[0], kb.at[r], sems.at[r, 0]).start()
                    pltpu.make_async_copy(ends[1], vb.at[r], sems.at[r, 1]).start()

    lane = lax.broadcasted_iota(jnp.int32, (ROWS, HEAD), 1)

    @pl.loop(0, GROUPS)
    def _(g):
        wait_slot(g, (qb, cb), gsems)
        for j in range(2):
            wait_slot(2 * g + j, (kb, vb), sems)
        stats = jnp.zeros((ROWS, HEAD), F32) if first else before[g]
        out = pl.ds(pl.multiple_of(g * ROWS, ROWS), ROWS)
        for base in range(0, cw // HEAD, HOME_GANG):
            span = [(h, j) for h in range(base, base + HOME_GANG) for j in range(2)]
            key = {(h, j): kb[2 * g + j, :, head(h)] for h, j in span}
            value = {(h, j): vb[2 * g + j, :, head(h)] for h, j in span}
            score = {(h, j): dot(qb[g, :, head(h)], key[h, j], 1, 1) * SCALE for h, j in span}
            slope = {(h, j): dot(cb[g, :, head(h)], value[h, j], 1, 1) for h, j in span}
            peak = {x: jnp.max(score[x], axis=1, keepdims=True) for x in span}
            e = {x: jnp.exp(score[x] - peak[x]) for x in span}
            total = {x: jnp.sum(e[x], axis=1, keepdims=True) for x in span}
            part = {x: dot(e[x].astype(BF16), value[x], 1, 0) for x in span}
            for h in range(base, base + HOME_GANG):
                top = jnp.maximum(peak[h, 0], peak[h, 1])
                scale = [jnp.exp(peak[h, j] - top) for j in range(2)]
                below = scale[0] * total[h, 0] + scale[1] * total[h, 1]
                scale = [x / below for x in scale]
                mix = part[h, 0] * scale[0] + part[h, 1] * scale[1]
                att[out, head(h)] = mix.astype(BF16)
                delta = jnp.sum(cb[g, :, head(h)].astype(F32) * mix, axis=1, keepdims=True)
                where = col // HEAD + h
                stats = jnp.where(lane == where, top + jnp.log(below), stats)
                stats = jnp.where(lane == HEADS + where, delta, stats)
                both = None
                for j in range(2):
                    gs = (e[h, j] * scale[j] * (slope[h, j] - delta) * SCALE).astype(BF16)
                    one = dot(gs, key[h, j], 1, 0)
                    both = one if both is None else both + one
                gq[out, head(h)] = both.astype(BF16)
        res[g] = stats

    if last:
        for d in range(4):
            for s in range(2):
                backs[d][s] = res[pick[2 * d + s]]


def home(pick, place, want, q, c, keys, values, pairs, before, last, col, cw):
    tokens = GROUPS * ROWS
    small = shape((2, ROWS, HEAD), F32)
    every = shape((GROUPS, ROWS, HEAD), F32)
    first = before is None
    extra = [] if first else [whole(GROUPS, ROWS, HEAD), ANY]
    out_shape = (shape((tokens, WIDTH), BF16), shape((tokens, cw), BF16))
    out_specs = (pl.BlockSpec((tokens, cw), lambda i: (0, col // cw)), whole(tokens, cw))
    keep = [pltpu.VMEM((GROUPS, ROWS, HEAD), F32)]
    if last:
        out_shape += (small,) * 4
        out_specs += (whole(2, ROWS, HEAD),) * 4
    else:
        out_shape += (every,)
        out_specs += (whole(GROUPS, ROWS, HEAD),)
        keep = []
    body = functools.partial(home_kernel, col, cw, first, last)
    if not last:
        inner = body

        def body(*refs):
            n = 10 + len(extra)
            ins, att, gq, res, rest = refs[:n], refs[n], refs[n + 1], refs[n + 2], refs[n + 3 :]
            inner(*ins, att, gq, *rest[:4], res, *rest[4:])

    return pl.pallas_call(
        body,
        out_shape=out_shape,
        grid=(1,),
        in_specs=[SMEM] * 3 + [ANY] * 7 + extra,
        out_specs=out_specs,
        scratch_shapes=[
            pltpu.VMEM((GROUPS, ROWS, cw), BF16),
            pltpu.VMEM((GROUPS, ROWS, cw), BF16),
            pltpu.VMEM((2 * GROUPS, LEN, cw), BF16),
            pltpu.VMEM((2 * GROUPS, LEN, cw), BF16),
            *keep,
            pltpu.SemaphoreType.DMA((2 * GROUPS, 2)),
            pltpu.SemaphoreType.DMA((GROUPS, 2)),
        ],
        input_output_aliases={} if first else {11: 0},
        compiler_params=params(BIG),
        cost_estimate=cost(6 * 8 * ROWS * LEN * cw, 30 * LEN * cw, 6 * ROWS * cw),
        name="home",
    )(pick, place, want, q, c, keys, values, *pairs, *(() if first else before))


def terms_kernel(tw, *refs):
    pick, asked, refs = refs[0], refs[1:5], refs[5:]
    q, c, keys, values, back = refs[:4], refs[4:8], refs[8], refs[9], refs[10:14]
    dk, dv, rows, seen, qb, cb, bb = refs[14:]
    fill_rows(asked, rows)
    for b in range(STORED):
        seen[b] = 0
    base = pl.program_id(0) * (tw // HEAD)
    for k in range(SLOTS):
        d, s = divmod(k, 2)
        at = pick[k] if d == 0 else s
        qb[k] = q[d][at]
        cb[k] = c[d][at]
        bb[k] = jnp.transpose(pltpu.roll(back[d][s], (HEAD - base) % HEAD, 1))

    def one_slot(k, row, add):
        for first in range(0, tw // HEAD, GANG):
            span = range(first, first + GANG)
            qs = [qb[k, :, head(h)] for h in span]
            cs = [cb[k, :, head(h)] for h in span]
            scores = [dot(keys[row, :, head(h)], x, 1, 1) * SCALE for h, x in zip(span, qs)]
            slopes = [dot(values[row, :, head(h)], x, 1, 1) for h, x in zip(span, cs)]
            probs = [jnp.exp(x - bb[k, h : h + 1, :]) for h, x in zip(span, scores)]
            gs = [
                (x * (y - bb[k, HEADS + h : HEADS + h + 1, :]) * SCALE).astype(BF16)
                for h, x, y in zip(span, probs, slopes)
            ]
            kts = [dot(x, y, 1, 0) for x, y in zip(gs, qs)]
            vts = [dot(x.astype(BF16), y, 1, 0) for x, y in zip(probs, cs)]
            for h, kt, vt in zip(span, kts, vts):
                if add:
                    kt = kt.astype(BF16).astype(F32) + dk[row, :, head(h)].astype(F32)
                    vt = vt.astype(BF16).astype(F32) + dv[row, :, head(h)].astype(F32)
                dk[row, :, head(h)] = kt.astype(BF16)
                dv[row, :, head(h)] = vt.astype(BF16)

    @pl.loop(0, SLOTS)
    def _(k):
        row = jnp.maximum(rows[k], 0)
        valid = rows[k] >= 0

        @pl.when(valid & (seen[row] == 0))
        def _():
            one_slot(k, row, False)

        @pl.when(valid & (seen[row] > 0))
        def _():
            one_slot(k, row, True)

        seen[row] = seen[row] + valid.astype(jnp.int32)

    for b in range(STORED):

        @pl.when(seen[b] == 0)
        def _(b=b):
            dk[b] = jnp.zeros((LEN, tw), BF16)
            dv[b] = jnp.zeros((LEN, tw), BF16)


def terms(pick, asked, q, c, keys, values, back):
    full = shape((STORED, LEN, WIDTH), BF16)
    tw = TWIDTH

    def part(x):
        return pl.BlockSpec((x.shape[0], x.shape[1], tw), lambda i: (0, 0, i))

    return pl.pallas_call(
        functools.partial(terms_kernel, tw),
        out_shape=(full,) * 2,
        grid=(WIDTH // tw,),
        in_specs=[SMEM] * 5 + [part(x) for x in (*q, *c, keys, values)] + [whole(2, ROWS, HEAD)] * 4,
        out_specs=(part(keys),) * 2,
        scratch_shapes=[
            pltpu.SMEM((SLOTS,), jnp.int32),
            pltpu.SMEM((STORED,), jnp.int32),
            pltpu.VMEM((SLOTS, ROWS, tw), BF16),
            pltpu.VMEM((SLOTS, ROWS, tw), BF16),
            pltpu.VMEM((SLOTS, HEAD, ROWS), F32),
        ],
        compiler_params=params(BIG),
        cost_estimate=cost(SLOTS * 8 * ROWS * LEN * WIDTH, 44 * LEN * WIDTH, SLOTS * ROWS * WIDTH),
        name="terms",
    )(pick, *asked, *q, *c, keys, values, *back)


def grad_kernel(gq, w, *refs):
    part = dot(gq[...], w[...], 1, 1)
    if len(refs) == 2:
        part = part + refs[0][...]
    refs[-1][...] = part.astype(refs[-1].dtype)


def grad(gq, weights, before, last, col, cw):
    depth, step = weights.shape[0], GSTEP
    first = before is None
    block = pl.BlockSpec((GROUPS * ROWS, step), lambda i: (0, i))
    return pl.pallas_call(
        grad_kernel,
        out_shape=shape((GROUPS * ROWS, depth), BF16 if last else F32),
        grid=(depth // step,),
        in_specs=[whole(GROUPS * ROWS, cw), pl.BlockSpec((step, cw), lambda i: (i, col // cw))]
        + ([] if first else [block]),
        out_specs=block,
        compiler_params=params(BIG),
        cost_estimate=cost(2 * 192 * depth * cw, 2 * depth * (384 + cw)),
        name="grad",
    )(gq, weights, *(() if first else (before,)))


def shift(x, d):
    return lax.ppermute(x, "enc", [(i, (i + d) % 4) for i in range(4)])


def to_owner(pieces):
    return [shift(x, d + 1) for d, x in enumerate(pieces)]


def to_home(pieces):
    return [shift(x, -(d + 1)) for d, x in enumerate(pieces)]


def after(values, *done):
    return lax.optimization_barrier((values, done))[0]


def per_device(hidden, query_weight, keys, values, owner, row, cotangent):
    me = lax.axis_index("enc").astype(jnp.int32).reshape(1)
    weights = lax.all_gather(query_weight, "fsdp", axis=0, tiled=True)
    pick, want, place = route(me, jnp.concatenate([owner, row], axis=1))
    cot = cotangent.reshape(GROUPS, ROWS, WIDTH)
    asked = [want] + to_owner([want] * 3)
    c = [cot] + to_owner(after(spread(pick, cot), asked[1]))
    sent = [collect(asked, keys, values, col, cw) for col, cw in PARTS]
    pairs = [to_home(after(pieces, c)) for pieces in sent]
    q, *sends = query(pick, hidden, weights)
    before, grad_hidden = None, None
    for (col, cw), pair in zip(PARTS, pairs):
        last = col + cw == WIDTH
        attended, gq, *back = home(pick, place, want, q, cot, keys, values, pair, before, last, col, cw)
        if before is None:
            qs = [q] + to_owner(after(sends, gq))
        before = (back[0], attended)
        grad_hidden = grad(gq, weights, grad_hidden, last, col, cw)
    back = [back[0]] + to_owner(back[1:])
    grad_keys, grad_values = terms(pick, asked, qs, c, keys, values, back)
    return attended, grad_hidden, grad_keys, grad_values


def solution(mesh):
    rows = P(("enc", "fsdp"), None)
    blocks = P(("enc", "fsdp"), None, None)
    return jax.shard_map(
        per_device,
        mesh=mesh,
        in_specs=(rows, P("fsdp", None), blocks, blocks, rows, rows, rows),
        out_specs=(rows, rows, blocks, blocks),
        check_vma=False,
    )
```

```python
import functools
import math

import jax
import jax.numpy as jnp
from jax import lax
from jax.experimental import pallas as pl
from jax.experimental.pallas import tpu as pltpu
from jax.sharding import PartitionSpec as P

HEAD = 128
LEN = 128
ROWS = 64
GROUPS = 3
STORED = 6
SLOTS = 8
WIDTH = 2048
SCALE = 1.0 / math.sqrt(HEAD)
F32 = jnp.float32
BF16 = jnp.bfloat16
ANY = pl.BlockSpec(memory_space=pltpu.HBM)
SMEM = pl.BlockSpec(memory_space=pltpu.SMEM)
VMEM = pl.BlockSpec(memory_space=pltpu.VMEM)


def whole(*dims):
    return pl.BlockSpec(dims, lambda i: (0,) * len(dims))


TWIDTH = 1024
GANG = 8
HOME_GANG = 4
PARTS = ((0, 1536), (1536, 512))
HEADS = 16
BIG = 58
QSTEP = 512
GSTEP = 1024


def params(mib):
    return pltpu.CompilerParams(vmem_limit_bytes=mib << 20)


def cost(flops, data, exps=0):
    return pl.CostEstimate(flops=int(flops), bytes_accessed=int(data), transcendentals=int(exps))


def shape(dims, dtype):
    return jax.ShapeDtypeStruct(dims, dtype)


def dot(a, b, ca, cb):
    return lax.dot_general(a, b, (((ca,), (cb,)), ((), ())), preferred_element_type=F32)


def head(h):
    return slice(h * HEAD, (h + 1) * HEAD)


def route_kernel(me, table, pick, want, place, count):
    for k in range(SLOTS):
        pick[k] = 0
        want[k] = -1
    for d in range(4):
        count[d] = 0
    for g in range(GROUPS):
        for j in range(2):
            d = (table[g, j] - me[0] + 4) % 4
            k = d * 2 + jnp.minimum(count[d], 1)
            count[d] = count[d] + 1
            pick[k] = g
            want[k] = table[g, 2 + j]
            place[g * 2 + j] = k


def route(me, table):
    return pl.pallas_call(
        route_kernel,
        out_shape=(shape((SLOTS,), jnp.int32), shape((SLOTS,), jnp.int32), shape((SLOTS,), jnp.int32)),
        in_specs=[SMEM] * 2,
        out_specs=(SMEM, SMEM, SMEM),
        scratch_shapes=[pltpu.SMEM((4,), jnp.int32)],
        name="route",
    )(me, table)


def spread_kernel(pick, cot, *outs):
    for d in range(1, 4):
        for s in range(2):
            outs[d - 1][s] = cot[pick[2 * d + s]]


def spread(pick, cot):
    one = shape((2, ROWS, WIDTH), BF16)
    return pl.pallas_call(
        spread_kernel,
        out_shape=(one,) * 3,
        grid=(1,),
        in_specs=[SMEM, whole(GROUPS, ROWS, WIDTH)],
        out_specs=(whole(2, ROWS, WIDTH),) * 3,
        compiler_params=params(BIG),
        cost_estimate=cost(1, 20 * ROWS * WIDTH),
        name="spread",
    )(pick, cot)


def query_kernel(pick, hid, w, q, s1, s2, s3):
    part = dot(hid[...], w[...], 1, 0)
    for g in range(GROUPS):
        q[g] = part[g * ROWS : (g + 1) * ROWS].astype(BF16)
    for d, out in ((1, s1), (2, s2), (3, s3)):
        for s in range(2):
            out[s] = q[pick[2 * d + s]]


def query(pick, hidden, weights):
    depth = hidden.shape[1]
    piece = shape((2, ROWS, WIDTH), BF16)
    block = pl.BlockSpec((2, ROWS, QSTEP), lambda i: (0, 0, i))
    return pl.pallas_call(
        query_kernel,
        out_shape=(shape((GROUPS, ROWS, WIDTH), BF16), piece, piece, piece),
        grid=(WIDTH // QSTEP,),
        in_specs=[
            SMEM,
            whole(GROUPS * ROWS, depth),
            pl.BlockSpec((depth, QSTEP), lambda i: (0, i)),
        ],
        out_specs=(pl.BlockSpec((GROUPS, ROWS, QSTEP), lambda i: (0, 0, i)), block, block, block),
        compiler_params=params(BIG),
        cost_estimate=cost(2 * 192 * depth * WIDTH, 2 * depth * (192 + WIDTH)),
        name="query",
    )(pick, hidden, weights)


def rows_of(k, asked):
    d, s = divmod(k, 2)
    return asked[d][2 * d + s]


def fill_rows(asked, rows):
    for k in range(SLOTS):
        rows[k] = rows_of(k, asked)


def wait_slot(k, bufs, sems):
    for n, buf in enumerate(bufs):
        pltpu.make_async_copy(buf.at[k], buf.at[k], sems.at[k, n]).wait()


def collect_kernel(col, cw, *refs):
    asked, tables, outs, buf, sems, osems = refs[:4], refs[4:6], refs[6:9], refs[9], refs[10], refs[11]
    loads, stores = [], []
    for k in range(2, SLOTS):
        d, s = divmod(k, 2)
        row = jnp.maximum(rows_of(k, asked), 0)
        for n in range(2):
            here = buf.at[k - 2, n]
            loads.append(pltpu.make_async_copy(tables[n].at[row, :, pl.ds(col, cw)], here, sems.at[k - 2, n]))
            stores.append(pltpu.make_async_copy(here, outs[d - 1].at[s, n], osems.at[k - 2, n]))
    for one in loads:
        one.start()
    for one, two in zip(loads, stores):
        one.wait()
        two.start()
    for one in stores:
        one.wait()


def collect(asked, keys, values, col, cw):
    one = shape((2, 2, LEN, cw), BF16)
    return pl.pallas_call(
        functools.partial(collect_kernel, col, cw),
        out_shape=(one,) * 3,
        in_specs=[SMEM] * 4 + [ANY] * 2,
        out_specs=(ANY,) * 3,
        scratch_shapes=[
            pltpu.VMEM((SLOTS - 2, 2, LEN, cw), BF16),
            pltpu.SemaphoreType.DMA((SLOTS - 2, 2)),
            pltpu.SemaphoreType.DMA((SLOTS - 2, 2)),
        ],
        compiler_params=params(BIG),
        cost_estimate=cost(1, 48 * LEN * cw),
        name="collect",
    )(*asked, keys, values)


def home_kernel(col, cw, first, last, *refs):
    pick, place, want, q, c, keys, values = refs[:7]
    pairs, refs = refs[7:10], refs[10:]
    if not first:
        before, refs = refs[0], refs[2:]
    att, gq, refs = refs[0], refs[1], refs[2:]
    if last:
        backs, refs = refs[:4], refs[4:]
    qb, cb, kb, vb, res, sems, gsems = refs
    cols = pl.ds(col, cw)
    for g in range(GROUPS):
        pltpu.make_async_copy(q.at[g, :, cols], qb.at[g], gsems.at[g, 0]).start()
        pltpu.make_async_copy(c.at[g, :, cols], cb.at[g], gsems.at[g, 1]).start()
        for r in (2 * g, 2 * g + 1):
            at = place[r]
            for d in range(4):

                @pl.when(at // 2 == d)
                def _(r=r, d=d, at=at):
                    if d == 0:
                        s = jnp.maximum(want[at], 0)
                        ends = keys.at[s, :, cols], values.at[s, :, cols]
                    else:
                        ends = pairs[d - 1].at[at - 2 * d, 0], pairs[d - 1].at[at - 2 * d, 1]
                    pltpu.make_async_copy(ends[0], kb.at[r], sems.at[r, 0]).start()
                    pltpu.make_async_copy(ends[1], vb.at[r], sems.at[r, 1]).start()

    lane = lax.broadcasted_iota(jnp.int32, (ROWS, HEAD), 1)

    @pl.loop(0, GROUPS)
    def _(g):
        wait_slot(g, (qb, cb), gsems)
        for j in range(2):
            wait_slot(2 * g + j, (kb, vb), sems)
        stats = jnp.zeros((ROWS, HEAD), F32) if first else before[g]
        out = pl.ds(pl.multiple_of(g * ROWS, ROWS), ROWS)
        for base in range(0, cw // HEAD, HOME_GANG):
            span = [(h, j) for h in range(base, base + HOME_GANG) for j in range(2)]
            key = {(h, j): kb[2 * g + j, :, head(h)] for h, j in span}
            value = {(h, j): vb[2 * g + j, :, head(h)] for h, j in span}
            score = {(h, j): dot(qb[g, :, head(h)], key[h, j], 1, 1) * SCALE for h, j in span}
            slope = {(h, j): dot(cb[g, :, head(h)], value[h, j], 1, 1) for h, j in span}
            peak = {x: jnp.max(score[x], axis=1, keepdims=True) for x in span}
            e = {x: jnp.exp(score[x] - peak[x]) for x in span}
            total = {x: jnp.sum(e[x], axis=1, keepdims=True) for x in span}
            part = {x: dot(e[x].astype(BF16), value[x], 1, 0) for x in span}
            for h in range(base, base + HOME_GANG):
                top = jnp.maximum(peak[h, 0], peak[h, 1])
                scale = [jnp.exp(peak[h, j] - top) for j in range(2)]
                below = scale[0] * total[h, 0] + scale[1] * total[h, 1]
                scale = [x / below for x in scale]
                mix = part[h, 0] * scale[0] + part[h, 1] * scale[1]
                att[out, head(h)] = mix.astype(BF16)
                delta = jnp.sum(cb[g, :, head(h)].astype(F32) * mix, axis=1, keepdims=True)
                where = col // HEAD + h
                stats = jnp.where(lane == where, top + jnp.log(below), stats)
                stats = jnp.where(lane == HEADS + where, delta, stats)
                both = None
                for j in range(2):
                    gs = (e[h, j] * scale[j] * (slope[h, j] - delta) * SCALE).astype(BF16)
                    one = dot(gs, key[h, j], 1, 0)
                    both = one if both is None else both + one
                gq[out, head(h)] = both.astype(BF16)
        res[g] = stats

    if last:
        for d in range(4):
            for s in range(2):
                backs[d][s] = res[pick[2 * d + s]]


def home(pick, place, want, q, c, keys, values, pairs, before, last, col, cw):
    tokens = GROUPS * ROWS
    small = shape((2, ROWS, HEAD), F32)
    every = shape((GROUPS, ROWS, HEAD), F32)
    first = before is None
    extra = [] if first else [whole(GROUPS, ROWS, HEAD), ANY]
    out_shape = (shape((tokens, WIDTH), BF16), shape((tokens, cw), BF16))
    out_specs = (pl.BlockSpec((tokens, cw), lambda i: (0, col // cw)), whole(tokens, cw))
    keep = [pltpu.VMEM((GROUPS, ROWS, HEAD), F32)]
    if last:
        out_shape += (small,) * 4
        out_specs += (whole(2, ROWS, HEAD),) * 4
    else:
        out_shape += (every,)
        out_specs += (whole(GROUPS, ROWS, HEAD),)
        keep = []
    body = functools.partial(home_kernel, col, cw, first, last)
    if not last:
        inner = body

        def body(*refs):
            n = 10 + len(extra)
            ins, att, gq, res, rest = refs[:n], refs[n], refs[n + 1], refs[n + 2], refs[n + 3 :]
            inner(*ins, att, gq, *rest[:4], res, *rest[4:])

    return pl.pallas_call(
        body,
        out_shape=out_shape,
        grid=(1,),
        in_specs=[SMEM] * 3 + [ANY] * 7 + extra,
        out_specs=out_specs,
        scratch_shapes=[
            pltpu.VMEM((GROUPS, ROWS, cw), BF16),
            pltpu.VMEM((GROUPS, ROWS, cw), BF16),
            pltpu.VMEM((2 * GROUPS, LEN, cw), BF16),
            pltpu.VMEM((2 * GROUPS, LEN, cw), BF16),
            *keep,
            pltpu.SemaphoreType.DMA((2 * GROUPS, 2)),
            pltpu.SemaphoreType.DMA((GROUPS, 2)),
        ],
        input_output_aliases={} if first else {11: 0},
        compiler_params=params(BIG),
        cost_estimate=cost(6 * 8 * ROWS * LEN * cw, 30 * LEN * cw, 6 * ROWS * cw),
        name="home",
    )(pick, place, want, q, c, keys, values, *pairs, *(() if first else before))


def terms_kernel(tw, *refs):
    pick, asked, refs = refs[0], refs[1:5], refs[5:]
    q, c, keys, values, back = refs[:4], refs[4:8], refs[8], refs[9], refs[10:14]
    dk, dv, rows, seen, qb, cb, bb = refs[14:]
    fill_rows(asked, rows)
    for b in range(STORED):
        seen[b] = 0
    base = pl.program_id(0) * (tw // HEAD)
    for k in range(SLOTS):
        d, s = divmod(k, 2)
        at = pick[k] if d == 0 else s
        qb[k] = q[d][at]
        cb[k] = c[d][at]
        bb[k] = jnp.transpose(pltpu.roll(back[d][s], (HEAD - base) % HEAD, 1))

    def one_slot(k, row, add):
        for first in range(0, tw // HEAD, GANG):
            span = range(first, first + GANG)
            qs = [qb[k, :, head(h)] for h in span]
            cs = [cb[k, :, head(h)] for h in span]
            scores = [dot(keys[row, :, head(h)], x, 1, 1) * SCALE for h, x in zip(span, qs)]
            slopes = [dot(values[row, :, head(h)], x, 1, 1) for h, x in zip(span, cs)]
            probs = [jnp.exp(x - bb[k, h : h + 1, :]) for h, x in zip(span, scores)]
            gs = [
                (x * (y - bb[k, HEADS + h : HEADS + h + 1, :]) * SCALE).astype(BF16)
                for h, x, y in zip(span, probs, slopes)
            ]
            kts = [dot(x, y, 1, 0) for x, y in zip(gs, qs)]
            vts = [dot(x.astype(BF16), y, 1, 0) for x, y in zip(probs, cs)]
            for h, kt, vt in zip(span, kts, vts):
                if add:
                    kt = kt.astype(BF16).astype(F32) + dk[row, :, head(h)].astype(F32)
                    vt = vt.astype(BF16).astype(F32) + dv[row, :, head(h)].astype(F32)
                dk[row, :, head(h)] = kt.astype(BF16)
                dv[row, :, head(h)] = vt.astype(BF16)

    @pl.loop(0, SLOTS)
    def _(k):
        row = jnp.maximum(rows[k], 0)
        valid = rows[k] >= 0

        @pl.when(valid & (seen[row] == 0))
        def _():
            one_slot(k, row, False)

        @pl.when(valid & (seen[row] > 0))
        def _():
            one_slot(k, row, True)

        seen[row] = seen[row] + valid.astype(jnp.int32)

    for b in range(STORED):

        @pl.when(seen[b] == 0)
        def _(b=b):
            dk[b] = jnp.zeros((LEN, tw), BF16)
            dv[b] = jnp.zeros((LEN, tw), BF16)


def terms(pick, asked, q, c, keys, values, back):
    full = shape((STORED, LEN, WIDTH), BF16)
    tw = TWIDTH

    def part(x):
        return pl.BlockSpec((x.shape[0], x.shape[1], tw), lambda i: (0, 0, i))

    return pl.pallas_call(
        functools.partial(terms_kernel, tw),
        out_shape=(full,) * 2,
        grid=(WIDTH // tw,),
        in_specs=[SMEM] * 5 + [part(x) for x in (*q, *c, keys, values)] + [whole(2, ROWS, HEAD)] * 4,
        out_specs=(part(keys),) * 2,
        scratch_shapes=[
            pltpu.SMEM((SLOTS,), jnp.int32),
            pltpu.SMEM((STORED,), jnp.int32),
            pltpu.VMEM((SLOTS, ROWS, tw), BF16),
            pltpu.VMEM((SLOTS, ROWS, tw), BF16),
            pltpu.VMEM((SLOTS, HEAD, ROWS), F32),
        ],
        compiler_params=params(BIG),
        cost_estimate=cost(SLOTS * 8 * ROWS * LEN * WIDTH, 44 * LEN * WIDTH, SLOTS * ROWS * WIDTH),
        name="terms",
    )(pick, *asked, *q, *c, keys, values, *back)


def grad_kernel(gq, w, *refs):
    part = dot(gq[...], w[...], 1, 1)
    if len(refs) == 2:
        part = part + refs[0][...]
    refs[-1][...] = part.astype(refs[-1].dtype)


def grad(gq, weights, before, last, col, cw):
    depth, step = weights.shape[0], GSTEP
    first = before is None
    block = pl.BlockSpec((GROUPS * ROWS, step), lambda i: (0, i))
    return pl.pallas_call(
        grad_kernel,
        out_shape=shape((GROUPS * ROWS, depth), BF16 if last else F32),
        grid=(depth // step,),
        in_specs=[whole(GROUPS * ROWS, cw), pl.BlockSpec((step, cw), lambda i: (i, col // cw))]
        + ([] if first else [block]),
        out_specs=block,
        compiler_params=params(BIG),
        cost_estimate=cost(2 * 192 * depth * cw, 2 * depth * (384 + cw)),
        name="grad",
    )(gq, weights, *(() if first else (before,)))


def shift(x, d):
    return lax.ppermute(x, "enc", [(i, (i + d) % 4) for i in range(4)])


def to_owner(pieces):
    return [shift(x, d + 1) for d, x in enumerate(pieces)]


def to_home(pieces):
    return [shift(x, -(d + 1)) for d, x in enumerate(pieces)]


def after(values, *done):
    return lax.optimization_barrier((values, done))[0]


def per_device(hidden, query_weight, keys, values, owner, row, cotangent):
    me = lax.axis_index("enc").astype(jnp.int32).reshape(1)
    weights = lax.all_gather(query_weight, "fsdp", axis=0, tiled=True)
    pick, want, place = route(me, jnp.concatenate([owner, row], axis=1))
    cot = cotangent.reshape(GROUPS, ROWS, WIDTH)
    asked = [want] + to_owner([want] * 3)
    c = [cot] + to_owner(after(spread(pick, cot), asked[1]))
    sent = [collect(asked, keys, values, col, cw) for col, cw in PARTS]
    q, *sends = query(pick, hidden, weights)
    pairs = [to_home(after(sent[0], c)), to_home([*after(sent[1][:2], c), after(sent[1][2], c, q)])]
    before, grad_hidden = None, None
    for (col, cw), pair in zip(PARTS, pairs):
        last = col + cw == WIDTH
        attended, gq, *back = home(pick, place, want, q, cot, keys, values, pair, before, last, col, cw)
        if before is None:
            qs = [q] + to_owner(after(sends, gq))
        before = (back[0], attended)
        grad_hidden = grad(gq, weights, grad_hidden, last, col, cw)
    back = [back[0]] + to_owner(back[1:])
    grad_keys, grad_values = terms(pick, asked, qs, c, keys, values, back)
    return attended, grad_hidden, grad_keys, grad_values


def solution(mesh):
    rows = P(("enc", "fsdp"), None)
    blocks = P(("enc", "fsdp"), None, None)
    return jax.shard_map(
        per_device,
        mesh=mesh,
        in_specs=(rows, P("fsdp", None), blocks, blocks, rows, rows, rows),
        out_specs=(rows, rows, blocks, blocks),
        check_vma=False,
    )
```

```python
import functools
import math

import jax
import jax.numpy as jnp
from jax import lax
from jax.experimental import pallas as pl
from jax.experimental.pallas import tpu as pltpu
from jax.sharding import PartitionSpec as P

HEAD = 128
LEN = 128
ROWS = 64
GROUPS = 3
STORED = 6
SLOTS = 8
WIDTH = 2048
SCALE = 1.0 / math.sqrt(HEAD)
F32 = jnp.float32
BF16 = jnp.bfloat16
ANY = pl.BlockSpec(memory_space=pltpu.HBM)
SMEM = pl.BlockSpec(memory_space=pltpu.SMEM)
VMEM = pl.BlockSpec(memory_space=pltpu.VMEM)


def whole(*dims):
    return pl.BlockSpec(dims, lambda i: (0,) * len(dims))


TWIDTH = 1024
GANG = 8
HOME_GANG = 4
PARTS = ((0, 1536), (1536, 512))
HEADS = 16
BIG = 58
QSTEP = 512
GSTEP = 1024


def params(mib):
    return pltpu.CompilerParams(vmem_limit_bytes=mib << 20)


def cost(flops, data, exps=0):
    return pl.CostEstimate(flops=int(flops), bytes_accessed=int(data), transcendentals=int(exps))


def shape(dims, dtype):
    return jax.ShapeDtypeStruct(dims, dtype)


def dot(a, b, ca, cb):
    return lax.dot_general(a, b, (((ca,), (cb,)), ((), ())), preferred_element_type=F32)


def head(h):
    return slice(h * HEAD, (h + 1) * HEAD)


def route_kernel(me, table, pick, want, place, count):
    for k in range(SLOTS):
        pick[k] = 0
        want[k] = -1
    for d in range(4):
        count[d] = 0
    for g in range(GROUPS):
        for j in range(2):
            d = (table[g, j] - me[0] + 4) % 4
            k = d * 2 + jnp.minimum(count[d], 1)
            count[d] = count[d] + 1
            pick[k] = g
            want[k] = table[g, 2 + j]
            place[g * 2 + j] = k


def route(me, table):
    return pl.pallas_call(
        route_kernel,
        out_shape=(shape((SLOTS,), jnp.int32), shape((SLOTS,), jnp.int32), shape((SLOTS,), jnp.int32)),
        in_specs=[SMEM] * 2,
        out_specs=(SMEM, SMEM, SMEM),
        scratch_shapes=[pltpu.SMEM((4,), jnp.int32)],
        name="route",
    )(me, table)


def spread_kernel(pick, cot, *outs):
    for d in range(1, 4):
        for s in range(2):
            outs[d - 1][s] = cot[pick[2 * d + s]]


def spread(pick, cot):
    one = shape((2, ROWS, WIDTH), BF16)
    return pl.pallas_call(
        spread_kernel,
        out_shape=(one,) * 3,
        grid=(1,),
        in_specs=[SMEM, whole(GROUPS, ROWS, WIDTH)],
        out_specs=(whole(2, ROWS, WIDTH),) * 3,
        compiler_params=params(BIG),
        cost_estimate=cost(1, 20 * ROWS * WIDTH),
        name="spread",
    )(pick, cot)


def query_kernel(pick, hid, w, q, s1, s2, s3):
    part = dot(hid[...], w[...], 1, 0)
    for g in range(GROUPS):
        q[g] = part[g * ROWS : (g + 1) * ROWS].astype(BF16)
    for d, out in ((1, s1), (2, s2), (3, s3)):
        for s in range(2):
            out[s] = q[pick[2 * d + s]]


def query(pick, hidden, weights):
    depth = hidden.shape[1]
    piece = shape((2, ROWS, WIDTH), BF16)
    block = pl.BlockSpec((2, ROWS, QSTEP), lambda i: (0, 0, i))
    return pl.pallas_call(
        query_kernel,
        out_shape=(shape((GROUPS, ROWS, WIDTH), BF16), piece, piece, piece),
        grid=(WIDTH // QSTEP,),
        in_specs=[
            SMEM,
            whole(GROUPS * ROWS, depth),
            pl.BlockSpec((depth, QSTEP), lambda i: (0, i)),
        ],
        out_specs=(pl.BlockSpec((GROUPS, ROWS, QSTEP), lambda i: (0, 0, i)), block, block, block),
        compiler_params=params(BIG),
        cost_estimate=cost(2 * 192 * depth * WIDTH, 2 * depth * (192 + WIDTH)),
        name="query",
    )(pick, hidden, weights)


def rows_of(k, asked):
    d, s = divmod(k, 2)
    return asked[d][2 * d + s]


def fill_rows(asked, rows):
    for k in range(SLOTS):
        rows[k] = rows_of(k, asked)


def wait_slot(k, bufs, sems):
    for n, buf in enumerate(bufs):
        pltpu.make_async_copy(buf.at[k], buf.at[k], sems.at[k, n]).wait()


def collect_kernel(col, cw, *refs):
    asked, tables, outs, buf, sems, osems = refs[:4], refs[4:6], refs[6:9], refs[9], refs[10], refs[11]
    loads, stores = [], []
    for k in range(2, SLOTS):
        d, s = divmod(k, 2)
        row = jnp.maximum(rows_of(k, asked), 0)
        for n in range(2):
            here = buf.at[k - 2, n]
            loads.append(pltpu.make_async_copy(tables[n].at[row, :, pl.ds(col, cw)], here, sems.at[k - 2, n]))
            stores.append(pltpu.make_async_copy(here, outs[d - 1].at[s, n], osems.at[k - 2, n]))
    for one in loads:
        one.start()
    for one, two in zip(loads, stores):
        one.wait()
        two.start()
    for one in stores:
        one.wait()


def collect(asked, keys, values, col, cw):
    one = shape((2, 2, LEN, cw), BF16)
    return pl.pallas_call(
        functools.partial(collect_kernel, col, cw),
        out_shape=(one,) * 3,
        in_specs=[SMEM] * 4 + [ANY] * 2,
        out_specs=(ANY,) * 3,
        scratch_shapes=[
            pltpu.VMEM((SLOTS - 2, 2, LEN, cw), BF16),
            pltpu.SemaphoreType.DMA((SLOTS - 2, 2)),
            pltpu.SemaphoreType.DMA((SLOTS - 2, 2)),
        ],
        compiler_params=params(BIG),
        cost_estimate=cost(1, 48 * LEN * cw),
        name="collect",
    )(*asked, keys, values)


def home_kernel(col, cw, first, last, *refs):
    pick, place, want, me, q, c, keys, values = refs[:8]
    pairs, refs = refs[8:11], refs[11:]
    if not first:
        before, refs = refs[0], refs[2:]
    att, gq, refs = refs[0], refs[1], refs[2:]
    if last:
        backs, refs = refs[0], refs[1:]
    qb, cb, kb, vb, res, sems, gsems = refs
    cols = pl.ds(col, cw)
    for g in range(GROUPS):
        pltpu.make_async_copy(q.at[g, :, cols], qb.at[g], gsems.at[g, 0]).start()
        pltpu.make_async_copy(c.at[g, :, cols], cb.at[g], gsems.at[g, 1]).start()
        for r in (2 * g, 2 * g + 1):
            at = place[r]
            for d in range(4):

                @pl.when(at // 2 == d)
                def _(r=r, d=d, at=at):
                    if d == 0:
                        s = jnp.maximum(want[at], 0)
                        ends = keys.at[s, :, cols], values.at[s, :, cols]
                    else:
                        ends = pairs[d - 1].at[at - 2 * d, 0], pairs[d - 1].at[at - 2 * d, 1]
                    pltpu.make_async_copy(ends[0], kb.at[r], sems.at[r, 0]).start()
                    pltpu.make_async_copy(ends[1], vb.at[r], sems.at[r, 1]).start()

    lane = lax.broadcasted_iota(jnp.int32, (ROWS, HEAD), 1)

    @pl.loop(0, GROUPS)
    def _(g):
        wait_slot(g, (qb, cb), gsems)
        for j in range(2):
            wait_slot(2 * g + j, (kb, vb), sems)
        stats = jnp.zeros((ROWS, HEAD), F32) if first else before[g]
        out = pl.ds(pl.multiple_of(g * ROWS, ROWS), ROWS)
        for base in range(0, cw // HEAD, HOME_GANG):
            span = [(h, j) for h in range(base, base + HOME_GANG) for j in range(2)]
            key = {(h, j): kb[2 * g + j, :, head(h)] for h, j in span}
            value = {(h, j): vb[2 * g + j, :, head(h)] for h, j in span}
            score = {(h, j): dot(qb[g, :, head(h)], key[h, j], 1, 1) * SCALE for h, j in span}
            slope = {(h, j): dot(cb[g, :, head(h)], value[h, j], 1, 1) for h, j in span}
            peak = {x: jnp.max(score[x], axis=1, keepdims=True) for x in span}
            e = {x: jnp.exp(score[x] - peak[x]) for x in span}
            total = {x: jnp.sum(e[x], axis=1, keepdims=True) for x in span}
            part = {x: dot(e[x].astype(BF16), value[x], 1, 0) for x in span}
            for h in range(base, base + HOME_GANG):
                top = jnp.maximum(peak[h, 0], peak[h, 1])
                scale = [jnp.exp(peak[h, j] - top) for j in range(2)]
                below = scale[0] * total[h, 0] + scale[1] * total[h, 1]
                scale = [x / below for x in scale]
                mix = part[h, 0] * scale[0] + part[h, 1] * scale[1]
                att[out, head(h)] = mix.astype(BF16)
                delta = jnp.sum(cb[g, :, head(h)].astype(F32) * mix, axis=1, keepdims=True)
                where = col // HEAD + h
                stats = jnp.where(lane == where, top + jnp.log(below), stats)
                stats = jnp.where(lane == HEADS + where, delta, stats)
                both = None
                for j in range(2):
                    gs = (e[h, j] * scale[j] * (slope[h, j] - delta) * SCALE).astype(BF16)
                    one = dot(gs, key[h, j], 1, 0)
                    both = one if both is None else both + one
                gq[out, head(h)] = both.astype(BF16)
        res[g] = stats

    if last:
        for d in range(4):
            for s in range(2):
                backs[(me[0] + d) % 4, s] = res[pick[2 * d + s]]


def home(pick, place, want, me, q, c, keys, values, pairs, before, last, col, cw):
    tokens = GROUPS * ROWS
    small = shape((4, 2, ROWS, HEAD), F32)
    every = shape((GROUPS, ROWS, HEAD), F32)
    first = before is None
    extra = [] if first else [whole(GROUPS, ROWS, HEAD), ANY]
    out_shape = (shape((tokens, WIDTH), BF16), shape((tokens, cw), BF16))
    out_specs = (pl.BlockSpec((tokens, cw), lambda i: (0, col // cw)), whole(tokens, cw))
    keep = [pltpu.VMEM((GROUPS, ROWS, HEAD), F32)]
    if last:
        out_shape += (small,)
        out_specs += (whole(4, 2, ROWS, HEAD),)
    else:
        out_shape += (every,)
        out_specs += (whole(GROUPS, ROWS, HEAD),)
        keep = []
    body = functools.partial(home_kernel, col, cw, first, last)
    if not last:
        inner = body

        def body(*refs):
            n = 11 + len(extra)
            ins, att, gq, res, rest = refs[:n], refs[n], refs[n + 1], refs[n + 2], refs[n + 3 :]
            inner(*ins, att, gq, *rest[:4], res, *rest[4:])

    return pl.pallas_call(
        body,
        out_shape=out_shape,
        grid=(1,),
        in_specs=[SMEM] * 4 + [ANY] * 7 + extra,
        out_specs=out_specs,
        scratch_shapes=[
            pltpu.VMEM((GROUPS, ROWS, cw), BF16),
            pltpu.VMEM((GROUPS, ROWS, cw), BF16),
            pltpu.VMEM((2 * GROUPS, LEN, cw), BF16),
            pltpu.VMEM((2 * GROUPS, LEN, cw), BF16),
            *keep,
            pltpu.SemaphoreType.DMA((2 * GROUPS, 2)),
            pltpu.SemaphoreType.DMA((GROUPS, 2)),
        ],
        input_output_aliases={} if first else {12: 0},
        compiler_params=params(BIG),
        cost_estimate=cost(6 * 8 * ROWS * LEN * cw, 30 * LEN * cw, 6 * ROWS * cw),
        name="home",
    )(pick, place, want, me, q, c, keys, values, *pairs, *(() if first else before))


def terms_kernel(tw, *refs):
    me, pick, asked, refs = refs[0], refs[1], refs[2:6], refs[6:]
    q, c, keys, values, back = refs[:4], refs[4:8], refs[8], refs[9], refs[10]
    dk, dv, rows, seen, qb, cb, bb = refs[11:]
    fill_rows(asked, rows)
    for b in range(STORED):
        seen[b] = 0
    base = pl.program_id(0) * (tw // HEAD)
    for k in range(SLOTS):
        d, s = divmod(k, 2)
        at = pick[k] if d == 0 else s
        qb[k] = q[d][at]
        cb[k] = c[d][at]
        bb[k] = jnp.transpose(pltpu.roll(back[(me[0] + 4 - d) % 4, s], (HEAD - base) % HEAD, 1))

    def one_slot(k, row, add):
        for first in range(0, tw // HEAD, GANG):
            span = range(first, first + GANG)
            qs = [qb[k, :, head(h)] for h in span]
            cs = [cb[k, :, head(h)] for h in span]
            scores = [dot(keys[row, :, head(h)], x, 1, 1) * SCALE for h, x in zip(span, qs)]
            slopes = [dot(values[row, :, head(h)], x, 1, 1) for h, x in zip(span, cs)]
            probs = [jnp.exp(x - bb[k, h : h + 1, :]) for h, x in zip(span, scores)]
            gs = [
                (x * (y - bb[k, HEADS + h : HEADS + h + 1, :]) * SCALE).astype(BF16)
                for h, x, y in zip(span, probs, slopes)
            ]
            kts = [dot(x, y, 1, 0) for x, y in zip(gs, qs)]
            vts = [dot(x.astype(BF16), y, 1, 0) for x, y in zip(probs, cs)]
            for h, kt, vt in zip(span, kts, vts):
                if add:
                    kt = kt.astype(BF16).astype(F32) + dk[row, :, head(h)].astype(F32)
                    vt = vt.astype(BF16).astype(F32) + dv[row, :, head(h)].astype(F32)
                dk[row, :, head(h)] = kt.astype(BF16)
                dv[row, :, head(h)] = vt.astype(BF16)

    @pl.loop(0, SLOTS)
    def _(k):
        row = jnp.maximum(rows[k], 0)
        valid = rows[k] >= 0

        @pl.when(valid & (seen[row] == 0))
        def _():
            one_slot(k, row, False)

        @pl.when(valid & (seen[row] > 0))
        def _():
            one_slot(k, row, True)

        seen[row] = seen[row] + valid.astype(jnp.int32)

    for b in range(STORED):

        @pl.when(seen[b] == 0)
        def _(b=b):
            dk[b] = jnp.zeros((LEN, tw), BF16)
            dv[b] = jnp.zeros((LEN, tw), BF16)


def terms(me, pick, asked, q, c, keys, values, back):
    full = shape((STORED, LEN, WIDTH), BF16)
    tw = TWIDTH

    def part(x):
        return pl.BlockSpec((x.shape[0], x.shape[1], tw), lambda i: (0, 0, i))

    return pl.pallas_call(
        functools.partial(terms_kernel, tw),
        out_shape=(full,) * 2,
        grid=(WIDTH // tw,),
        in_specs=[SMEM] * 6 + [part(x) for x in (*q, *c, keys, values)] + [whole(4, 2, ROWS, HEAD)],
        out_specs=(part(keys),) * 2,
        scratch_shapes=[
            pltpu.SMEM((SLOTS,), jnp.int32),
            pltpu.SMEM((STORED,), jnp.int32),
            pltpu.VMEM((SLOTS, ROWS, tw), BF16),
            pltpu.VMEM((SLOTS, ROWS, tw), BF16),
            pltpu.VMEM((SLOTS, HEAD, ROWS), F32),
        ],
        compiler_params=params(BIG),
        cost_estimate=cost(SLOTS * 8 * ROWS * LEN * WIDTH, 44 * LEN * WIDTH, SLOTS * ROWS * WIDTH),
        name="terms",
    )(me, pick, *asked, *q, *c, keys, values, back)


def grad_kernel(gq, w, *refs):
    part = dot(gq[...], w[...], 1, 1)
    if len(refs) == 2:
        part = part + refs[0][...]
    refs[-1][...] = part.astype(refs[-1].dtype)


def grad(gq, weights, before, last, col, cw):
    depth, step = weights.shape[0], GSTEP
    first = before is None
    block = pl.BlockSpec((GROUPS * ROWS, step), lambda i: (0, i))
    return pl.pallas_call(
        grad_kernel,
        out_shape=shape((GROUPS * ROWS, depth), BF16 if last else F32),
        grid=(depth // step,),
        in_specs=[whole(GROUPS * ROWS, cw), pl.BlockSpec((step, cw), lambda i: (i, col // cw))]
        + ([] if first else [block]),
        out_specs=block,
        compiler_params=params(BIG),
        cost_estimate=cost(2 * 192 * depth * cw, 2 * depth * (384 + cw)),
        name="grad",
    )(gq, weights, *(() if first else (before,)))


def shift(x, d):
    return lax.ppermute(x, "enc", [(i, (i + d) % 4) for i in range(4)])


def to_owner(pieces):
    return [shift(x, d + 1) for d, x in enumerate(pieces)]


def to_home(pieces):
    return [shift(x, -(d + 1)) for d, x in enumerate(pieces)]


def after(values, *done):
    return lax.optimization_barrier((values, done))[0]


def per_device(hidden, query_weight, keys, values, owner, row, cotangent):
    me = lax.axis_index("enc").astype(jnp.int32).reshape(1)
    weights = lax.all_gather(query_weight, "fsdp", axis=0, tiled=True)
    pick, want, place = route(me, jnp.concatenate([owner, row], axis=1))
    cot = cotangent.reshape(GROUPS, ROWS, WIDTH)
    asked = [want] + to_owner([want] * 3)
    c = [cot] + to_owner(after(spread(pick, cot), asked[1]))
    sent = [collect(asked, keys, values, col, cw) for col, cw in PARTS]
    q, *sends = query(pick, hidden, weights)
    pairs = [to_home(after(sent[0], c)), to_home([*after(sent[1][:2], c), after(sent[1][2], c, q)])]
    before, grad_hidden = None, None
    for (col, cw), pair in zip(PARTS, pairs):
        last = col + cw == WIDTH
        attended, gq, *back = home(pick, place, want, me, q, cot, keys, values, pair, before, last, col, cw)
        partial = grad_hidden
        grad_hidden = grad(gq, weights, partial, last, col, cw)
        if before is None:
            qs = [q] + to_owner(after(sends, pairs[1], grad_hidden))
            before = after((back[0], attended), grad_hidden)
    back = lax.all_to_all(back[0], "enc", split_axis=0, concat_axis=0, tiled=True)
    grad_keys, grad_values = terms(me, pick, asked, qs, c, keys, values, back)
    return attended, grad_hidden, grad_keys, grad_values


def solution(mesh):
    rows = P(("enc", "fsdp"), None)
    blocks = P(("enc", "fsdp"), None, None)
    return jax.shard_map(
        per_device,
        mesh=mesh,
        in_specs=(rows, P("fsdp", None), blocks, blocks, rows, rows, rows),
        out_specs=(rows, rows, blocks, blocks),
        check_vma=False,
    )
```

```python
import functools
import math

import jax
import jax.numpy as jnp
from jax import lax
from jax.experimental import pallas as pl
from jax.experimental.pallas import tpu as pltpu
from jax.sharding import PartitionSpec as P

HEAD = 128
LEN = 128
ROWS = 64
GROUPS = 3
STORED = 6
SLOTS = 8
WIDTH = 2048
SCALE = 1.0 / math.sqrt(HEAD)
F32 = jnp.float32
BF16 = jnp.bfloat16
ANY = pl.BlockSpec(memory_space=pltpu.HBM)
SMEM = pl.BlockSpec(memory_space=pltpu.SMEM)
VMEM = pl.BlockSpec(memory_space=pltpu.VMEM)


def whole(*dims):
    return pl.BlockSpec(dims, lambda i: (0,) * len(dims))


TWIDTH = 1024
GANG = 8
HOME_GANG = 4
PARTS = ((0, 1536), (1536, 512))
HEADS = 16
BIG = 58
QSTEP = 512
GSTEP = 1024


def params(mib):
    return pltpu.CompilerParams(vmem_limit_bytes=mib << 20)


def cost(flops, data, exps=0):
    return pl.CostEstimate(flops=int(flops), bytes_accessed=int(data), transcendentals=int(exps))


def shape(dims, dtype):
    return jax.ShapeDtypeStruct(dims, dtype)


def dot(a, b, ca, cb):
    return lax.dot_general(a, b, (((ca,), (cb,)), ((), ())), preferred_element_type=F32)


def head(h):
    return slice(h * HEAD, (h + 1) * HEAD)


def route_kernel(me, table, pick, want, place, count):
    for k in range(SLOTS):
        pick[k] = 0
        want[k] = -1
    for d in range(4):
        count[d] = 0
    for g in range(GROUPS):
        for j in range(2):
            d = (table[g, j] - me[0] + 4) % 4
            k = d * 2 + jnp.minimum(count[d], 1)
            count[d] = count[d] + 1
            pick[k] = g
            want[k] = table[g, 2 + j]
            place[g * 2 + j] = k


def route(me, table):
    return pl.pallas_call(
        route_kernel,
        out_shape=(shape((SLOTS,), jnp.int32), shape((SLOTS,), jnp.int32), shape((SLOTS,), jnp.int32)),
        in_specs=[SMEM] * 2,
        out_specs=(SMEM, SMEM, SMEM),
        scratch_shapes=[pltpu.SMEM((4,), jnp.int32)],
        name="route",
    )(me, table)


def spread_kernel(pick, cot, *outs):
    for d in range(1, 4):
        for s in range(2):
            outs[d - 1][s] = cot[pick[2 * d + s]]


def spread(pick, cot):
    one = shape((2, ROWS, WIDTH), BF16)
    return pl.pallas_call(
        spread_kernel,
        out_shape=(one,) * 3,
        grid=(1,),
        in_specs=[SMEM, whole(GROUPS, ROWS, WIDTH)],
        out_specs=(whole(2, ROWS, WIDTH),) * 3,
        compiler_params=params(BIG),
        cost_estimate=cost(1, 20 * ROWS * WIDTH),
        name="spread",
    )(pick, cot)


def query_kernel(pick, hid, w, q, s1, s2, s3):
    part = dot(hid[...], w[...], 1, 0)
    for g in range(GROUPS):
        q[g] = part[g * ROWS : (g + 1) * ROWS].astype(BF16)
    for d, out in ((1, s1), (2, s2), (3, s3)):
        for s in range(2):
            out[s] = q[pick[2 * d + s]]


def query(pick, hidden, weights):
    depth = hidden.shape[1]
    piece = shape((2, ROWS, WIDTH), BF16)
    block = pl.BlockSpec((2, ROWS, QSTEP), lambda i: (0, 0, i))
    return pl.pallas_call(
        query_kernel,
        out_shape=(shape((GROUPS, ROWS, WIDTH), BF16), piece, piece, piece),
        grid=(WIDTH // QSTEP,),
        in_specs=[
            SMEM,
            whole(GROUPS * ROWS, depth),
            pl.BlockSpec((depth, QSTEP), lambda i: (0, i)),
        ],
        out_specs=(pl.BlockSpec((GROUPS, ROWS, QSTEP), lambda i: (0, 0, i)), block, block, block),
        compiler_params=params(BIG),
        cost_estimate=cost(2 * 192 * depth * WIDTH, 2 * depth * (192 + WIDTH)),
        name="query",
    )(pick, hidden, weights)


def rows_of(k, asked):
    d, s = divmod(k, 2)
    return asked[d][2 * d + s]


def fill_rows(asked, rows):
    for k in range(SLOTS):
        rows[k] = rows_of(k, asked)


def wait_slot(k, bufs, sems):
    for n, buf in enumerate(bufs):
        pltpu.make_async_copy(buf.at[k], buf.at[k], sems.at[k, n]).wait()


def collect_kernel(col, cw, *refs):
    asked, tables, outs, buf, sems, osems = refs[:4], refs[4:6], refs[6:9], refs[9], refs[10], refs[11]
    loads, stores = [], []
    for k in range(2, SLOTS):
        d, s = divmod(k, 2)
        row = jnp.maximum(rows_of(k, asked), 0)
        for n in range(2):
            here = buf.at[k - 2, n]
            loads.append(pltpu.make_async_copy(tables[n].at[row, :, pl.ds(col, cw)], here, sems.at[k - 2, n]))
            stores.append(pltpu.make_async_copy(here, outs[d - 1].at[s, n], osems.at[k - 2, n]))
    for one in loads:
        one.start()
    for one, two in zip(loads, stores):
        one.wait()
        two.start()
    for one in stores:
        one.wait()


def collect(asked, keys, values, col, cw):
    one = shape((2, 2, LEN, cw), BF16)
    return pl.pallas_call(
        functools.partial(collect_kernel, col, cw),
        out_shape=(one,) * 3,
        in_specs=[SMEM] * 4 + [ANY] * 2,
        out_specs=(ANY,) * 3,
        scratch_shapes=[
            pltpu.VMEM((SLOTS - 2, 2, LEN, cw), BF16),
            pltpu.SemaphoreType.DMA((SLOTS - 2, 2)),
            pltpu.SemaphoreType.DMA((SLOTS - 2, 2)),
        ],
        compiler_params=params(BIG),
        cost_estimate=cost(1, 48 * LEN * cw),
        name="collect",
    )(*asked, keys, values)


def home_kernel(col, cw, first, last, *refs):
    pick, place, want, me, q, c, keys, values = refs[:8]
    pairs, refs = refs[8:11], refs[11:]
    if not first:
        before, refs = refs[0], refs[2:]
    att, gq, refs = refs[0], refs[1], refs[2:]
    if last:
        backs, refs = refs[0], refs[1:]
    qb, cb, kb, vb, res, sems, gsems = refs
    cols = pl.ds(col, cw)
    for g in range(GROUPS):
        pltpu.make_async_copy(q.at[g, :, cols], qb.at[g], gsems.at[g, 0]).start()
        pltpu.make_async_copy(c.at[g, :, cols], cb.at[g], gsems.at[g, 1]).start()
        for r in (2 * g, 2 * g + 1):
            at = place[r]
            for d in range(4):

                @pl.when(at // 2 == d)
                def _(r=r, d=d, at=at):
                    if d == 0:
                        s = jnp.maximum(want[at], 0)
                        ends = keys.at[s, :, cols], values.at[s, :, cols]
                    else:
                        ends = pairs[d - 1].at[at - 2 * d, 0], pairs[d - 1].at[at - 2 * d, 1]
                    pltpu.make_async_copy(ends[0], kb.at[r], sems.at[r, 0]).start()
                    pltpu.make_async_copy(ends[1], vb.at[r], sems.at[r, 1]).start()

    lane = lax.broadcasted_iota(jnp.int32, (ROWS, HEAD), 1)

    @pl.loop(0, GROUPS)
    def _(g):
        wait_slot(g, (qb, cb), gsems)
        for j in range(2):
            wait_slot(2 * g + j, (kb, vb), sems)
        stats = jnp.zeros((ROWS, HEAD), F32) if first else before[g]
        out = pl.ds(pl.multiple_of(g * ROWS, ROWS), ROWS)
        for base in range(0, cw // HEAD, HOME_GANG):
            span = [(h, j) for h in range(base, base + HOME_GANG) for j in range(2)]
            key = {(h, j): kb[2 * g + j, :, head(h)] for h, j in span}
            value = {(h, j): vb[2 * g + j, :, head(h)] for h, j in span}
            score = {(h, j): dot(qb[g, :, head(h)], key[h, j], 1, 1) * SCALE for h, j in span}
            slope = {(h, j): dot(cb[g, :, head(h)], value[h, j], 1, 1) for h, j in span}
            peak = {x: jnp.max(score[x], axis=1, keepdims=True) for x in span}
            e = {x: jnp.exp(score[x] - peak[x]) for x in span}
            total = {x: jnp.sum(e[x], axis=1, keepdims=True) for x in span}
            part = {x: dot(e[x].astype(BF16), value[x], 1, 0) for x in span}
            for h in range(base, base + HOME_GANG):
                top = jnp.maximum(peak[h, 0], peak[h, 1])
                scale = [jnp.exp(peak[h, j] - top) for j in range(2)]
                below = scale[0] * total[h, 0] + scale[1] * total[h, 1]
                scale = [x / below for x in scale]
                mix = part[h, 0] * scale[0] + part[h, 1] * scale[1]
                att[out, head(h)] = mix.astype(BF16)
                delta = jnp.sum(cb[g, :, head(h)].astype(F32) * mix, axis=1, keepdims=True)
                where = col // HEAD + h
                stats = jnp.where(lane == where, top + jnp.log(below), stats)
                stats = jnp.where(lane == HEADS + where, delta, stats)
                both = None
                for j in range(2):
                    gs = (e[h, j] * scale[j] * (slope[h, j] - delta) * SCALE).astype(BF16)
                    one = dot(gs, key[h, j], 1, 0)
                    both = one if both is None else both + one
                gq[out, head(h)] = both.astype(BF16)
        res[g] = stats

    if last:
        for d in range(4):
            for s in range(2):
                backs[(me[0] + d) % 4, s] = res[pick[2 * d + s]]


def home(pick, place, want, me, q, c, keys, values, pairs, before, last, col, cw):
    tokens = GROUPS * ROWS
    small = shape((4, 2, ROWS, HEAD), F32)
    every = shape((GROUPS, ROWS, HEAD), F32)
    first = before is None
    extra = [] if first else [whole(GROUPS, ROWS, HEAD), ANY]
    out_shape = (shape((tokens, WIDTH), BF16), shape((tokens, cw), BF16))
    out_specs = (pl.BlockSpec((tokens, cw), lambda i: (0, col // cw)), whole(tokens, cw))
    keep = [pltpu.VMEM((GROUPS, ROWS, HEAD), F32)]
    if last:
        out_shape += (small,)
        out_specs += (whole(4, 2, ROWS, HEAD),)
    else:
        out_shape += (every,)
        out_specs += (whole(GROUPS, ROWS, HEAD),)
        keep = []
    body = functools.partial(home_kernel, col, cw, first, last)
    if not last:
        inner = body

        def body(*refs):
            n = 11 + len(extra)
            ins, att, gq, res, rest = refs[:n], refs[n], refs[n + 1], refs[n + 2], refs[n + 3 :]
            inner(*ins, att, gq, *rest[:4], res, *rest[4:])

    return pl.pallas_call(
        body,
        out_shape=out_shape,
        grid=(1,),
        in_specs=[SMEM] * 4 + [ANY] * 7 + extra,
        out_specs=out_specs,
        scratch_shapes=[
            pltpu.VMEM((GROUPS, ROWS, cw), BF16),
            pltpu.VMEM((GROUPS, ROWS, cw), BF16),
            pltpu.VMEM((2 * GROUPS, LEN, cw), BF16),
            pltpu.VMEM((2 * GROUPS, LEN, cw), BF16),
            *keep,
            pltpu.SemaphoreType.DMA((2 * GROUPS, 2)),
            pltpu.SemaphoreType.DMA((GROUPS, 2)),
        ],
        input_output_aliases={} if first else {12: 0},
        compiler_params=params(BIG),
        cost_estimate=cost(6 * 8 * ROWS * LEN * cw, 30 * LEN * cw, 6 * ROWS * cw),
        name="home",
    )(pick, place, want, me, q, c, keys, values, *pairs, *(() if first else before))


def terms_kernel(tw, *refs):
    me, pick, asked, refs = refs[0], refs[1], refs[2:6], refs[6:]
    q, c, keys, values, back = refs[:4], refs[4:8], refs[8], refs[9], refs[10]
    dk, dv, rows, seen, qb, cb, bb = refs[11:]
    fill_rows(asked, rows)
    for b in range(STORED):
        seen[b] = 0
    base = pl.program_id(0) * (tw // HEAD)
    for k in range(SLOTS):
        d, s = divmod(k, 2)
        at = pick[k] if d == 0 else s
        qb[k] = q[d][at]
        cb[k] = c[d][at]
        bb[k] = jnp.transpose(pltpu.roll(back[(me[0] + 4 - d) % 4, s], (HEAD - base) % HEAD, 1))

    def one_slot(k, row, add):
        for first in range(0, tw // HEAD, GANG):
            span = range(first, first + GANG)
            qs = [qb[k, :, head(h)] for h in span]
            cs = [cb[k, :, head(h)] for h in span]
            scores = [dot(keys[row, :, head(h)], x, 1, 1) * SCALE for h, x in zip(span, qs)]
            slopes = [dot(values[row, :, head(h)], x, 1, 1) for h, x in zip(span, cs)]
            probs = [jnp.exp(x - bb[k, h : h + 1, :]) for h, x in zip(span, scores)]
            gs = [
                (x * (y - bb[k, HEADS + h : HEADS + h + 1, :]) * SCALE).astype(BF16)
                for h, x, y in zip(span, probs, slopes)
            ]
            kts = [dot(x, y, 1, 0) for x, y in zip(gs, qs)]
            vts = [dot(x.astype(BF16), y, 1, 0) for x, y in zip(probs, cs)]
            for h, kt, vt in zip(span, kts, vts):
                if add:
                    kt = kt.astype(BF16).astype(F32) + dk[row, :, head(h)].astype(F32)
                    vt = vt.astype(BF16).astype(F32) + dv[row, :, head(h)].astype(F32)
                dk[row, :, head(h)] = kt.astype(BF16)
                dv[row, :, head(h)] = vt.astype(BF16)

    @pl.loop(0, SLOTS)
    def _(k):
        row = jnp.maximum(rows[k], 0)
        valid = rows[k] >= 0

        @pl.when(valid & (seen[row] == 0))
        def _():
            one_slot(k, row, False)

        @pl.when(valid & (seen[row] > 0))
        def _():
            one_slot(k, row, True)

        seen[row] = seen[row] + valid.astype(jnp.int32)

    for b in range(STORED):

        @pl.when(seen[b] == 0)
        def _(b=b):
            dk[b] = jnp.zeros((LEN, tw), BF16)
            dv[b] = jnp.zeros((LEN, tw), BF16)


def terms(me, pick, asked, q, c, keys, values, back):
    full = shape((STORED, LEN, WIDTH), BF16)
    tw = TWIDTH

    def part(x):
        return pl.BlockSpec((x.shape[0], x.shape[1], tw), lambda i: (0, 0, i))

    return pl.pallas_call(
        functools.partial(terms_kernel, tw),
        out_shape=(full,) * 2,
        grid=(WIDTH // tw,),
        in_specs=[SMEM] * 6 + [part(x) for x in (*q, *c, keys, values)] + [whole(4, 2, ROWS, HEAD)],
        out_specs=(part(keys),) * 2,
        scratch_shapes=[
            pltpu.SMEM((SLOTS,), jnp.int32),
            pltpu.SMEM((STORED,), jnp.int32),
            pltpu.VMEM((SLOTS, ROWS, tw), BF16),
            pltpu.VMEM((SLOTS, ROWS, tw), BF16),
            pltpu.VMEM((SLOTS, HEAD, ROWS), F32),
        ],
        compiler_params=params(BIG),
        cost_estimate=cost(SLOTS * 8 * ROWS * LEN * WIDTH, 44 * LEN * WIDTH, SLOTS * ROWS * WIDTH),
        name="terms",
    )(me, pick, *asked, *q, *c, keys, values, back)


def grad_kernel(gq, w, *refs):
    part = dot(gq[...], w[...], 1, 1)
    if len(refs) == 2:
        part = part + refs[0][...]
    refs[-1][...] = part.astype(refs[-1].dtype)


def grad(gq, weights, before, last, col, cw):
    depth, step = weights.shape[0], GSTEP
    first = before is None
    block = pl.BlockSpec((GROUPS * ROWS, step), lambda i: (0, i))
    return pl.pallas_call(
        grad_kernel,
        out_shape=shape((GROUPS * ROWS, depth), BF16 if last else F32),
        grid=(depth // step,),
        in_specs=[whole(GROUPS * ROWS, cw), pl.BlockSpec((step, cw), lambda i: (i, col // cw))]
        + ([] if first else [block]),
        out_specs=block,
        compiler_params=params(BIG),
        cost_estimate=cost(2 * 192 * depth * cw, 2 * depth * (384 + cw)),
        name="grad",
    )(gq, weights, *(() if first else (before,)))


def shift(x, d):
    return lax.ppermute(x, "enc", [(i, (i + d) % 4) for i in range(4)])


def to_owner(pieces):
    return [shift(x, d + 1) for d, x in enumerate(pieces)]


def to_home(pieces):
    return [shift(x, -(d + 1)) for d, x in enumerate(pieces)]


def after(values, *done):
    return lax.optimization_barrier((values, done))[0]


def per_device(hidden, query_weight, keys, values, owner, row, cotangent):
    me = lax.axis_index("enc").astype(jnp.int32).reshape(1)
    weights = lax.all_gather(query_weight, "fsdp", axis=0, tiled=True)
    pick, want, place = route(me, jnp.concatenate([owner, row], axis=1))
    cot = cotangent.reshape(GROUPS, ROWS, WIDTH)
    asked = [want] + to_owner([want] * 3)
    c = [cot] + to_owner(after(spread(pick, cot), asked[1]))
    sent = [collect(asked, keys, values, col, cw) for col, cw in PARTS]
    q, *sends = query(pick, hidden, weights)
    pairs = [to_home(after(sent[0], c)), to_home([*after(sent[1][:2], c), after(sent[1][2], c, q)])]
    before, grad_hidden = None, None
    for (col, cw), pair in zip(PARTS, pairs):
        last = col + cw == WIDTH
        attended, gq, *back = home(pick, place, want, me, q, cot, keys, values, pair, before, last, col, cw)
        partial = grad_hidden
        grad_hidden = grad(gq, weights, partial, last, col, cw)
        if before is None:
            qs = [q] + to_owner(after(sends, grad_hidden))
            before = after((back[0], attended), grad_hidden)
    back = lax.all_to_all(back[0], "enc", split_axis=0, concat_axis=0, tiled=True)
    grad_keys, grad_values = terms(me, pick, asked, qs, c, keys, values, back)
    return attended, grad_hidden, grad_keys, grad_values


def solution(mesh):
    rows = P(("enc", "fsdp"), None)
    blocks = P(("enc", "fsdp"), None, None)
    return jax.shard_map(
        per_device,
        mesh=mesh,
        in_specs=(rows, P("fsdp", None), blocks, blocks, rows, rows, rows),
        out_specs=(rows, rows, blocks, blocks),
        check_vma=False,
    )
```
